768 devices in a mesh: az: 32 (over y, z_lo), rad: 12 (over x, z_hi), dep: 2 (over core).
Axes of the slice: x: 4, y: 8, z: 12 (z_hi: 3, z_lo: 4; z = z_hi * 4 + z_lo), core: 2. Of those that a mesh axis runs over, the one named last changes fastest.
Arguments:
- displacement: float32 [3, 96, 32, 4096], P(None, 'rad', 'dep', 'az'), may hold values from -3 to 3
- velocity: float32 [3, 96, 32, 4096], P(None, 'rad', 'dep', 'az'), may hold values from -4 to 4
- modulus: float32 [96, 32, 4096], P('rad', 'dep', 'az'), may hold values from 0.5 to 2
- classes: int32 [96, 32, 4096], P('rad', 'dep', 'az'), may hold values from 0 to 7
- bond_integrity: float32 [32, 96, 32, 4096], P(None, 'rad', 'dep', 'az'), may hold values from 0 to 1, as said below
- densities: float32 [8], replicated, may hold values from 0.5 to 2
- adjoint_disp: float32 [3, 96, 32, 4096], P(None, 'rad', 'dep', 'az'), may hold values from -6 to 6
- adjoint_vel: float32 [3, 96, 32, 4096], P(None, 'rad', 'dep', 'az'), may hold values from -6 to 6
Outputs:
- moved_disp: float32 [3, 96, 32, 4096], P(None, 'rad', 'dep', 'az')
- new_velocity: float32 [3, 96, 32, 4096], P(None, 'rad', 'dep', 'az')
- grad_disp: float32 [3, 96, 32, 4096], P(None, 'rad', 'dep', 'az')
- grad_vel: float32 [3, 96, 32, 4096], P(None, 'rad', 'dep', 'az')
- grad_modulus: float32 [96, 32, 4096], P('rad', 'dep', 'az')
The draws below stay inside these ranges and needn't reach their ends.
Inputs may be any that keep to these rules, and one draw needn't show every extreme that they name: The two cells of a bond agree: bond_integrity[k, x] equals bond_integrity[31 - k, x + xi_k], with the azimuth index wrapping modulo 4096.
All inputs are finite; a program needn't handle non-finite values.
Results may differ from the reference program's by a relative error of at most 0.00002.
Values sent between devices are 32-bit elements; how exact they have to be, the bound alone decides.
A program may use at most 64 MiB of HBM per device.

```python
import math
import jax
import jax.numpy as jnp

NCLASS = 8
NR = 96
NZ = 32
NA = 4096


BOND_OFFSETS = [(along_rad, along_dep, along_az) for along_rad in range(-2, 3) for along_dep in range(-2, 3) for along_az in range(-2, 3) if 0 < along_rad * along_rad + along_dep * along_dep + along_az * along_az <= 4]


def draw_bond_integrity(key, part):
    number = len(BOND_OFFSETS)
    layers = [None] * number
    for position in range(number // 2):
        offset = BOND_OFFSETS[position]
        partner = number - 1 - position
        bond_key = jax.random.fold_in(key, position)
        broken = jax.random.randint(jax.random.fold_in(bond_key, 1), (NR, NZ, NA), 0, 4) == 0
        level = jax.random.uniform(jax.random.fold_in(bond_key, 2), (NR, NZ, NA), jnp.float32, 0.5, 1.0)
        value = jnp.where(broken, 0.0, level).astype(jnp.float32)
        layers[position] = value
        layers[partner] = jnp.roll(value, offset, axis=(0, 1, 2))
    return jnp.stack(layers)


def touch_ends(entries, own_key, least, high):
    index_at = [jax.random.randint(jax.random.fold_in(own_key, axis), (), 0, length) for axis, length in enumerate(entries.shape)]
    main_axis = entries.shape.index(max(entries.shape))
    next_to = index_at[:main_axis] + [(index_at[main_axis] + 1) % entries.shape[main_axis]] + index_at[main_axis + 1:]
    return entries.at[tuple(index_at)].set(least).at[tuple(next_to)].set(high)


def steps_of(stream_key, extent, cuts, least, largest):
    def one(axis_at, blocks):
        heights = jax.random.uniform(jax.random.fold_in(jax.random.fold_in(stream_key, 6), axis_at), (blocks,), jnp.float32, least / len(cuts), largest / len(cuts))
        return jnp.repeat(jnp.exp(heights), extent[axis_at] // blocks).reshape((-1,) + (1,) * (len(extent) - axis_at - 1))

    loudness = one(*cuts[0])
    for cut in cuts[1:]:
        loudness = loudness * one(*cut)
    return loudness


def noise(key, extent, scale, bound, shards=(), kind=jnp.bfloat16):
    values = jax.random.normal(key, extent, jnp.float32) * scale
    if len(shards) > 0:
        values = steps_of(key, extent, shards, -0.22, 0.18) * values
    return jnp.clip(values, min=-bound, max=bound).astype(kind)


def setup_inputs(seed: int = 0) -> dict:
    seeds = jax.random.split(jax.random.key(seed), 9)
    displacement = noise(seeds[0], (3, NR, NZ, NA), 0.5, 3.0, ((1, 12), (2, 2), (3, 32)), jnp.float32)
    velocity = noise(seeds[1], (3, NR, NZ, NA), 1.0, 4.0, ((1, 12), (2, 2), (3, 32)), jnp.float32)
    modulus = jnp.clip(jnp.exp(math.log(2.0) - 1.3862944 * jax.random.uniform(seeds[2], (NR, NZ, NA), jnp.float32) ** steps_of(seeds[2], (NR, NZ, NA), ((0, 12), (1, 2), (2, 32)), -0.2, 0.2)), 0.5, 2.0)
    classes = touch_ends(jax.random.randint(seeds[3], (NR, NZ, NA), 0, NCLASS), jax.random.fold_in(seeds[3], 1), 0, NCLASS - 1).astype(jnp.int32)
    bond_integrity = draw_bond_integrity(jax.random.fold_in(seeds[8], 71), 0)
    densities = jnp.clip(jnp.exp(jax.random.uniform(seeds[5], (NCLASS,), jnp.float32, math.log(0.5), math.log(2.0))), 0.5, 2.0)
    adjoint_disp = noise(seeds[6], (3, NR, NZ, NA), 1.0, 6.0, ((1, 12), (2, 2), (3, 32)), jnp.float32)
    adjoint_vel = noise(seeds[7], (3, NR, NZ, NA), 1.0, 6.0, ((1, 12), (2, 2), (3, 32)), jnp.float32)
    return {"displacement": displacement, "velocity": velocity, "modulus": modulus, "classes": classes, "bond_integrity": bond_integrity, "densities": densities, "adjoint_disp": adjoint_disp, "adjoint_vel": adjoint_vel}


SOFTEN = 0.5
TIME_STEP = 0.5
BOND_OFFSETS = [(along_rad, along_dep, along_az) for along_rad in range(-2, 3) for along_dep in range(-2, 3) for along_az in range(-2, 3) if 0 < along_rad * along_rad + along_dep * along_dep + along_az * along_az <= 4]

def widen(field):
    leading = [(0, 0)] * (field.ndim - 3)
    looped = jnp.pad(field, leading + [(0, 0), (0, 0), (2, 2)], mode='wrap')
    return jnp.pad(looped, leading + [(2, 2), (2, 2), (0, 0)])

def neighbour(wide, offset, shape):
    return wide[..., 2 + offset[0]:2 + offset[0] + shape[0], 2 + offset[1]:2 + offset[1] + shape[1], 2 + offset[2]:2 + offset[2] + shape[2]]

def project(offset, near, centre):
    total = jnp.zeros(centre.shape[1:], jnp.float32)
    for component in range(3):
        if offset[component] != 0:
            total = total + offset[component] * (near[component] - centre[component])
    return total

def sweep(centre, centre_wide, modulus, modulus_wide, bond_integrity, adjoint, adjoint_wide, with_force):
    shape = modulus.shape
    force_parts = [jnp.zeros(shape, jnp.float32) for component in range(3)]
    turned_parts = [jnp.zeros(shape, jnp.float32) for component in range(3)]
    sensitivity = jnp.zeros(shape, jnp.float32)
    for position, offset in enumerate(BOND_OFFSETS):
        length_sq = float(offset[0] * offset[0] + offset[1] * offset[1] + offset[2] * offset[2])
        length = math.sqrt(length_sq)
        intact = bond_integrity[position]
        near_mod = neighbour(modulus_wide, offset, shape)
        stretch = project(offset, neighbour(centre_wide, offset, shape), centre) / length_sq
        bent = jnp.tanh(stretch / SOFTEN)
        total_mod = modulus + near_mod
        bond_mod = intact * (2.0 * modulus * near_mod / total_mod)
        if with_force:
            push = bond_mod * (SOFTEN / length) * bent
            for component in range(3):
                if offset[component] != 0:
                    force_parts[component] = force_parts[component] + offset[component] * push
        if adjoint is not None:
            pull = project(offset, neighbour(adjoint_wide, offset, shape), adjoint)
            stiff = bond_mod * (1.0 - bent * bent) * pull / (length_sq * length)
            for component in range(3):
                if offset[component] != 0:
                    turned_parts[component] = turned_parts[component] + offset[component] * stiff
            sensitivity = sensitivity - intact * (SOFTEN / length) * bent * pull * (2.0 * near_mod * near_mod / (total_mod * total_mod))
    return (jnp.stack(force_parts), jnp.stack(turned_parts), sensitivity)

def reference(displacement, velocity, modulus, classes, bond_integrity, densities, adjoint_disp, adjoint_vel):
    density = jnp.take(densities, classes)
    modulus_wide = widen(modulus)
    disp_wide = widen(displacement)
    force_start = sweep(displacement, disp_wide, modulus, modulus_wide, bond_integrity, None, None, True)[0]
    accel_start = force_start / density
    moved_disp = displacement + TIME_STEP * velocity + 0.5 * TIME_STEP * TIME_STEP * accel_start
    carried = 0.5 * TIME_STEP * adjoint_vel / density
    force_moved, turned_moved, sens_moved = sweep(moved_disp, widen(moved_disp), modulus, modulus_wide, bond_integrity, carried, widen(carried), True)
    new_velocity = velocity + 0.5 * TIME_STEP * (accel_start + force_moved / density)
    total_moved = adjoint_disp + turned_moved
    grad_vel = adjoint_vel + TIME_STEP * total_moved
    back = (0.5 * TIME_STEP * adjoint_vel + 0.5 * TIME_STEP * TIME_STEP * total_moved) / density
    unused, turned_start, sens_start = sweep(displacement, disp_wide, modulus, modulus_wide, bond_integrity, back, widen(back), False)
    grad_disp = total_moved + turned_start
    grad_modulus = sens_moved + sens_start
    return (moved_disp, new_velocity, grad_disp, grad_vel, grad_modulus)
```

```python
import math

import jax
import jax.numpy as jnp
from jax import lax
from jax.experimental import pallas as pl
from jax.experimental.pallas import tpu as pltpu
from jax.sharding import PartitionSpec as P

BOND_OFFSETS = [
    (p, q, r)
    for p in range(-2, 3)
    for q in range(-2, 3)
    for r in range(-2, 3)
    if 0 < p * p + q * q + r * r <= 4
]
F32 = jnp.float32
NPL, NROW, NLANE = 8, 16, 128
DISP, CARRIED, MOVED, BACK = range(4)
SETS = 4
MESH = pl.DeviceIdType.MESH
NEIGHBOURS = [
    (da, dr, dd)
    for dd in (0, 1)
    for dr in (-1, 0, 1)
    for da in (-1, 0, 1)
    if (da, dr, dd) != (0, 0, 0)
]
MESSAGES = sorted(NEIGHBOURS, key=lambda n: (not (n[0] == 0 and n[2] == 0), abs(n[1])))
NEAR = [n for n in MESSAGES if n[1] == 0]
RADIAL = {
    side: [n for n in MESSAGES if n[1] == (-1 if side else 1)] for side in (0, 1)
}


def size_of(offset):
    length_sq = sum(o * o for o in offset)
    mult = max(abs(o) for o in offset)
    return mult, 2.0 * mult / length_sq, mult / math.sqrt(length_sq)


def signed(offset, parts):
    total = None
    for o, part in zip(offset, parts):
        if o != 0:
            if total is None:
                total = part if o > 0 else -part
            else:
                total = total + part if o > 0 else total - part
    return total


def add_signed(offset, parts, value):
    return [
        part if o == 0 else (part + value if o > 0 else part - value)
        for o, part in zip(offset, parts)
    ]


def kernel(
    disp_h,
    vel_h,
    mod_h,
    cls_h,
    bi_h,
    dens,
    adjd_h,
    adjv_h,
    moved_h,
    newv_h,
    gdisp_h,
    gvel_h,
    gmod_h,
    disp,
    vel,
    mod,
    cls,
    bi,
    adjd,
    adjv,
    rden,
    w,
    m,
    ecoef,
    gcoef,
    acoef,
    bcoef,
    xcoef,
    force1,
    force2,
    turn2,
    turn3,
    sens,
    o_newv,
    o_gvel,
    o_gdisp,
    o_gmod,
    pack,
    sd,
    se,
    sf,
    rp,
    rpr,
    rd,
    rf,
    rdr,
    re,
    rer,
    load_sem,
    store_sem,
    send_sem,
    recv_sem,
):
    az, rad, dep = lax.axis_index("az"), lax.axis_index("rad"), lax.axis_index("dep")
    naz, nrad = lax.axis_size("az"), lax.axis_size("rad")
    lane = lax.broadcasted_iota(jnp.int32, (NROW, NLANE), 1)
    lane8 = lax.broadcasted_iota(jnp.int32, (8, NLANE), 1)
    sub8 = lax.broadcasted_iota(jnp.int32, (8, NLANE), 0)

    def place(n):
        da, dr, dd = n
        return {
            "az": lax.rem(az + (da + naz), naz),
            "rad": lax.rem(rad + (dr + nrad), nrad),
            "dep": (1 - dep) if dd else dep,
        }

    barrier = pltpu.get_barrier_semaphore()
    for n in NEIGHBOURS:
        pl.semaphore_signal(barrier, inc=1, device_id=place(n), device_id_type=MESH)

    loads = {}
    for j, (name, src, dst) in enumerate(
        (
            ("disp", disp_h, disp),
            ("mod", mod_h, mod),
            ("cls", cls_h, cls),
            ("adjv", adjv_h, adjv),
            ("bi", bi_h, bi),
            ("vel", vel_h, vel),
            ("adjd", adjd_h, adjd),
        )
    ):
        loads[name] = pltpu.make_async_copy(src, dst, load_sem.at[j])
        loads[name].start()

    edge_row = 15 - 15 * dep
    second_row = 14 - 13 * dep
    halo_row = 8 + 16 - 17 * dep
    halo_row2 = 8 + 17 - 19 * dep
    blank = 24 * dep
    blank = pl.multiple_of(24 - 24 * (1 - dep), 8)

    def clear(ref):
        ref[:, pl.ds(blank, 8), :] = jnp.zeros((12, 8, NLANE), F32)
        for plane in (0, 1, 10, 11):
            ref[plane] = jnp.zeros((32, NLANE), F32)

    def clear_w(j, carry):
        clear(w.at[j])
        return carry

    def clear_m(j, carry):
        clear(m.at[j])
        return carry

    lax.fori_loop(0, SETS * 9, clear_w, 0)
    lax.fori_loop(0, 5, clear_m, 0)
    sd[...] = jnp.zeros(sd.shape, F32)
    pack[...] = jnp.zeros(pack.shape, F32)

    def chan(t, c, r):
        return w.at[t * 9 + c * 3 + 1 + r]

    def near(t, c, offset, i):
        p, q, r = offset
        if abs(r) == 2:
            return w[SETS * 9 + t * 2 + (r > 0), i + 2, 8:24, :]
        return w[t * 9 + c * 3 + 1 + r, i + (2 + p), 8 + q : 24 + q, :]

    def near_m(offset, i):
        p, q, r = offset
        return m[2 + r, i + (2 + p), 8 + q : 24 + q, :]

    def centre(t, i):
        return [w[t * 9 + c * 3 + 1, i + 2, 8:24, :] for c in range(3)]

    def project(t, offset, i, cen):
        parts = [near(t, c, offset, i) if offset[c] else None for c in range(3)]
        return signed(offset, parts) - signed(offset, cen)

    def pack_plane(t, i, with_mod):
        packed = pack[t]
        for c in range(4 if with_mod else 3):
            ref = m.at[2] if c == 3 else chan(t, c, 0)
            group = 4 * i + c
            rolled = pltpu.roll(ref[i + 2, 8:24, :], 4 * group + 2, 1)
            packed = jnp.where(lane // 4 == group, rolled, packed)
            sd[t, i, c : c + 1, :] = ref[i + 2, pl.ds(8 + edge_row, 1), :]
            if c in (1, 3):
                at = 4 if c == 1 else 5
                sd[t, i, at : at + 1, :] = ref[i + 2, pl.ds(8 + second_row, 1), :]
        pack[t] = packed

    def pack_faces(t, with_mod):
        packed = pack[t]
        for side in (0, 1):
            outer, inner = (9, 8) if side else (2, 3)
            for c in range(3):
                sf[side, t, c] = chan(t, c, 0)[outer, 8:24, :]
            sf[side, t, 3] = chan(t, 0, 0)[inner, 8:24, :]
            if with_mod:
                sf[side, t, 4] = m[2, outer, 8:24, :]
                sf[side, t, 5] = m[2, inner, 8:24, :]
            turned = pltpu.roll(packed, 16, 1) if side else packed
            for half in (0, 1):
                y = jnp.where(lane8 < 16, turned[8 * half : 8 * half + 8], 0.0)
                for bit in (1, 2, 4):
                    y = jnp.where((sub8 & bit) != 0, pltpu.roll(y, 16 * bit, 1), y)
                se[side, t, half : half + 1, :] = jnp.sum(y, axis=0, keepdims=True)

    def copies(phase):
        made = {}
        first, count = ((0, 2), (2, 1), (3, 1))[phase]
        sets = pl.ds(first, count)
        for j, n in enumerate(MESSAGES):
            da, dr, dd = n
            a = 0 if da == 1 else 1
            out = 1 if dr == 1 else 0
            r = 1 - out
            if da == 0 and dd == 0:
                planes = pl.ds(0, 6 if phase == 0 else 4)
                pair = sf.at[out, first, planes], rf.at[r, first, planes]
            elif da == 0 and dr == 0:
                pair = sd.at[sets], rd.at[sets]
            elif da == 0:
                plane = 7 if dr == 1 else 0
                rows = pl.ds(0, 4)
                pair = sd.at[sets, plane, rows], rdr.at[r, sets, rows]
            elif dr == 0 and dd == 0:
                pair = pack.at[sets], rp.at[a, sets]
            elif dr == 0:
                pair = pack.at[sets, pl.ds(edge_row, 1)], rpr.at[a, sets]
            elif dd == 0:
                pair = se.at[out, sets], re.at[a, r, sets]
            else:
                pair = se.at[out, sets, pl.ds(1 - dep, 1)], rer.at[a, r, sets]
            made[n] = pltpu.make_async_remote_copy(
                src_ref=pair[0],
                dst_ref=pair[1],
                send_sem=send_sem.at[phase * 17 + j],
                recv_sem=recv_sem.at[phase * 17 + j],
                device_id=place(n),
                device_id_type=MESH,
            )
        return made

    def carried_copies():
        made = {}
        for out in (0, 1):
            made[1 - out] = pltpu.make_async_remote_copy(
                src_ref=sf.at[out, CARRIED, pl.ds(0, 4)],
                dst_ref=rf.at[1 - out, CARRIED, pl.ds(0, 4)],
                send_sem=send_sem.at[51 + out],
                recv_sem=recv_sem.at[51 + out],
                device_id=place((0, 1 if out else -1, 0)),
                device_id_type=MESH,
            )
        return made

    def both(left, right, lanes):
        return jnp.where(lanes % 4 < 2, left, right)

    def shifted(value, edge, lanes, by):
        if by > 0:
            return pltpu.roll(jnp.where(lanes < by, edge, value), NLANE - by, 1)
        return pltpu.roll(jnp.where(lanes >= NLANE + by, edge, value), -by, 1)

    def spread(row, step, bits):
        y = jnp.broadcast_to(row, (8, NLANE))
        for bit in bits:
            turned = pltpu.roll(y, (NLANE - step * bit) % NLANE, 1)
            y = jnp.where((sub8 & bit) != 0, turned, y)
        return y

    def turn_left(value, by):
        return pltpu.roll(value, lax.rem(2 * NLANE - by, NLANE), 1)

    def take_own(t, with_mod):
        sides = both(rp[0, t], rp[1, t], lane)
        rows = spread(both(rpr[0, t], rpr[1, t], lane8[0:1]), 4, (1, 2))

        def plane(i, carry):
            for c in range(4 if with_mod else 3):
                ref = m.at[2] if c == 3 else chan(t, c, 0)
                value = ref[i + 2, 8:24, :]
                edge = turn_left(sides, 16 * i + (4 * c + 2))
                for r in (-1, 1):
                    to = m.at[2 + r] if c == 3 else chan(t, c, r)
                    to[i + 2, 8:24, :] = shifted(value, edge, lane, r)
                if c >= 2:
                    for r in (-2, 2):
                        to = m.at[2 + r] if c == 3 else w.at[SETS * 9 + t * 2 + (r > 0)]
                        to[i + 2, 8:24, :] = shifted(value, edge, lane, r)
            tile = rd[t, i]
            edge = turn_left(rows, 16 * i + 2)
            for r in (-1, 0, 1):
                moved = tile if r == 0 else shifted(tile, edge, lane8, r)
                for c in range(4 if with_mod else 3):
                    to = m.at[2 + r] if c == 3 else chan(t, c, r)
                    to[i + 2, pl.ds(halo_row, 1), :] = moved[c : c + 1]
            chan(t, 1, 0)[i + 2, pl.ds(halo_row2, 1), :] = tile[4:5]
            if with_mod:
                m[2, i + 2, pl.ds(halo_row2, 1), :] = tile[5:6]
            return carry

        lax.fori_loop(0, NPL, plane, 0)

    def take_radial(t, side, with_mod):
        at, far = (10, 11) if side else (1, 0)
        there = (rad < nrad - 1) if side else (rad > 0)
        present = jnp.where(there, 1.0, 0.0).astype(F32)
        edges = [
            spread(
                both(
                    re[0, side, t, h : h + 1, :], re[1, side, t, h : h + 1, :], lane8[0:1]
                ),
                16,
                (1, 2, 4),
            )
            for h in (0, 1)
        ]
        for c in range(4 if with_mod else 3):
            value = rf[side, t, 4 if c == 3 else c]
            turned = [pltpu.roll(e, NLANE - (4 * c + 2), 1) for e in edges]
            edge = jnp.concatenate(turned, axis=0)
            for r in (-1, 0, 1):
                new = value if r == 0 else shifted(value, edge, lane, r)
                if c == 3:
                    m[2 + r, at, 8:24, :] = new * present
                else:
                    chan(t, c, r)[at, 8:24, :] = new
        chan(t, 0, 0)[far, 8:24, :] = rf[side, t, 3]
        if with_mod:
            m[2, far, 8:24, :] = rf[side, t, 5] * present
        rows = spread(both(rer[0, side, t], rer[1, side, t], lane8[0:1]), 4, (1, 2))
        edge = turn_left(rows, 16 * 7 * dep + 2)
        tile = rdr[side, t]
        for r in (-1, 0, 1):
            moved = tile if r == 0 else shifted(tile, edge, lane8, r)
            for c in range(4 if with_mod else 3):
                if c == 3:
                    m[2 + r, at, pl.ds(halo_row, 1), :] = moved[3:4] * present
                else:
                    chan(t, c, r)[at, pl.ds(halo_row, 1), :] = moved[c : c + 1]

    def bond_first(offset, i, cen, cm, intact, forces):
        mult, kappa, scale = size_of(offset)
        nm = near_m(offset, i)
        half = cm * nm / (cm + nm)
        e = intact * half * scale
        bend = jnp.tanh(kappa * project(DISP, offset, i, cen))
        push = e * bend
        g = e * half
        return add_signed(offset, forces, push), (
            e,
            g,
            kappa * (e - push * bend),
            g * bend,
        )

    def bond_second(offset, i, cen, cen_z, e, g, forces, turns, total):
        kappa = size_of(offset)[1]
        bend = jnp.tanh(kappa * project(MOVED, offset, i, cen))
        pull = project(CARRIED, offset, i, cen_z)
        push = e * bend
        stiff = kappa * (e - push * bend) * pull
        forces = add_signed(offset, forces, push)
        turns = add_signed(offset, turns, stiff)
        return forces, turns, total + g * bend * pull

    def bond_third(offset, i, cen_z, a, b, turns, total):
        pull = project(BACK, offset, i, cen_z)
        return add_signed(offset, turns, a * pull), total + b * pull

    def zeros(count):
        return [jnp.zeros((NROW, NLANE), F32) for _ in range(count)]

    def crossing(side):
        sign = 1 if side else -1
        outer, inner = (7, 6) if side else (0, 1)
        found = [(outer, k) for k, o in enumerate(BOND_OFFSETS) if o[0] == sign]
        double = BOND_OFFSETS.index((2 * sign, 0, 0))
        return found + [(outer, double), (inner, double)]

    def cross_first(side):
        for j, (i, k) in enumerate(crossing(side)):
            offset = BOND_OFFSETS[k]
            forces = [force1[c, i] for c in range(3)]
            forces, made = bond_first(
                offset, i, centre(DISP, i), m[2, i + 2, 8:24, :], bi[k, i], forces
            )
            for c in range(3):
                if offset[c]:
                    force1[c, i] = forces[c]
            for n, value in enumerate(made):
                xcoef[n, side * 11 + j] = value

    def cross_second(side):
        for j, (i, k) in enumerate(crossing(side)):
            offset = BOND_OFFSETS[k]
            x = side * 11 + j
            forces, turns, total = bond_second(
                offset,
                i,
                centre(MOVED, i),
                centre(CARRIED, i),
                xcoef[0, x],
                xcoef[1, x],
                [force2[c, i] for c in range(3)],
                [turn2[c, i] for c in range(3)],
                sens[i],
            )
            for c in range(3):
                if offset[c]:
                    force2[c, i] = forces[c]
                    turn2[c, i] = turns[c]
            sens[i] = total

    def cross_third(side):
        for j, (i, k) in enumerate(crossing(side)):
            offset = BOND_OFFSETS[k]
            x = side * 11 + j
            turns, total = bond_third(
                offset,
                i,
                centre(BACK, i),
                xcoef[2, x],
                xcoef[3, x],
                [turn3[c, i] for c in range(3)],
                sens[i],
            )
            for c in range(3):
                if offset[c]:
                    turn3[c, i] = turns[c]
            sens[i] = total

    for name in ("disp", "mod", "cls", "adjv"):
        loads[name].wait()

    def begin(i, carry):
        kinds = cls[i]
        density = jnp.zeros((NROW, NLANE), F32)
        for level in range(8):
            density = jnp.where(kinds == level, dens[level], density)
        inverse = 1.0 / density
        rden[i] = inverse
        m[2, i + 2, 8:24, :] = mod[i]
        for c in range(3):
            chan(DISP, c, 0)[i + 2, 8:24, :] = disp[c, i]
            chan(CARRIED, c, 0)[i + 2, 8:24, :] = 0.25 * adjv[c, i] * inverse
        pack_plane(DISP, i, True)
        pack_plane(CARRIED, i, False)
        return carry

    lax.fori_loop(0, NPL, begin, 0)
    pack_faces(DISP, True)
    pack_faces(CARRIED, False)
    pl.semaphore_wait(barrier, len(NEIGHBOURS))
    sent = copies(0)
    for n in MESSAGES:
        sent[n].start()
    sent_carried = carried_copies()
    for side in (0, 1):
        sent_carried[side].start()
    for name in ("bi", "vel", "adjd"):
        loads[name].wait()
    for n in NEAR:
        sent[n].wait_recv()
    take_own(DISP, True)
    take_own(CARRIED, False)

    def sweep_first(i, carry):
        cen, cm, forces = centre(DISP, i), m[2, i + 2, 8:24, :], zeros(3)
        for k, offset in enumerate(BOND_OFFSETS):
            forces, made = bond_first(offset, i, cen, cm, bi[k, i], forces)
            for ref, value in zip((ecoef, gcoef, acoef, bcoef), made):
                ref[k, i] = value
        for c in range(3):
            force1[c, i] = forces[c]
        return carry

    lax.fori_loop(0, NPL, sweep_first, 0)

    def end_first(i):
        for c in range(3):
            accel = force1[c, i] * rden[i]
            moved = disp[c, i] + 0.5 * vel[c, i] + 0.125 * accel
            chan(MOVED, c, 0)[i + 2, 8:24, :] = moved
        pack_plane(MOVED, i, False)

    def inner_planes(step):
        def body(j, carry):
            step(j + 2)
            return carry

        lax.fori_loop(0, 4, body, 0)

    def outer_planes(step):
        def body(j, carry):
            step(j + 4 * (j // 2))
            return carry

        lax.fori_loop(0, 4, body, 0)

    inner_planes(end_first)
    for n in MESSAGES:
        sent[n].wait_send()
    for side in (0, 1):
        for n in RADIAL[side]:
            sent[n].wait_recv()
        take_radial(DISP, side, True)
        cross_first(side)
    outer_planes(end_first)
    pack_faces(MOVED, False)

    sent = copies(1)
    for n in MESSAGES:
        sent[n].start()
    moved_out = [
        pltpu.make_async_copy(
            chan(MOVED, c, 0).at[pl.ds(2, NPL), pl.ds(8, NROW)], moved_h.at[c], store_sem.at[c]
        )
        for c in range(3)
    ]
    for copy in moved_out:
        copy.start()
    for side in (0, 1):
        sent_carried[side].wait_recv()
        sent_carried[side].wait_send()
        take_radial(CARRIED, side, False)
    for n in NEAR:
        sent[n].wait_recv()
    take_own(MOVED, False)

    def sweep_second(i, carry):
        cen, cen_z = centre(MOVED, i), centre(CARRIED, i)
        forces, turns, total = zeros(3), zeros(3), zeros(1)[0]
        for k, offset in enumerate(BOND_OFFSETS):
            forces, turns, total = bond_second(
                offset, i, cen, cen_z, ecoef[k, i], gcoef[k, i], forces, turns, total
            )
        for c in range(3):
            force2[c, i] = forces[c]
            turn2[c, i] = turns[c]
        sens[i] = total
        return carry

    lax.fori_loop(0, NPL, sweep_second, 0)

    def end_second(i):
        for c in range(3):
            total = adjd[c, i] + turn2[c, i]
            turn2[c, i] = total
            back = (0.25 * adjv[c, i] + 0.125 * total) * rden[i]
            chan(BACK, c, 0)[i + 2, 8:24, :] = back
        pack_plane(BACK, i, False)

    inner_planes(end_second)
    for n in MESSAGES:
        sent[n].wait_send()
    for side in (0, 1):
        for n in RADIAL[side]:
            sent[n].wait_recv()
        take_radial(MOVED, side, False)
        cross_second(side)
    outer_planes(end_second)
    pack_faces(BACK, False)

    sent = copies(2)
    for n in MESSAGES:
        sent[n].start()

    def velocities(i, carry):
        for c in range(3):
            accel = (force1[c, i] + force2[c, i]) * rden[i]
            o_newv[c, i] = vel[c, i] + 0.25 * accel
            o_gvel[c, i] = adjv[c, i] + 0.5 * turn2[c, i]
        return carry

    lax.fori_loop(0, NPL, velocities, 0)
    outs = [
        pltpu.make_async_copy(o_newv, newv_h, store_sem.at[3]),
        pltpu.make_async_copy(o_gvel, gvel_h, store_sem.at[4]),
    ]
    for copy in outs:
        copy.start()
    for n in NEAR:
        sent[n].wait_recv()
    take_own(BACK, False)

    def sweep_third(i, carry):
        cen_z, turns, total = centre(BACK, i), zeros(3), sens[i]
        for k, offset in enumerate(BOND_OFFSETS):
            turns, total = bond_third(offset, i, cen_z, acoef[k, i], bcoef[k, i], turns, total)
        for c in range(3):
            turn3[c, i] = turns[c]
        sens[i] = total
        return carry

    lax.fori_loop(0, NPL, sweep_third, 0)
    for n in MESSAGES:
        sent[n].wait_send()
    for side in (0, 1):
        for n in RADIAL[side]:
            sent[n].wait_recv()
        take_radial(BACK, side, False)
        cross_third(side)

    def finish(i, carry):
        for c in range(3):
            o_gdisp[c, i] = turn2[c, i] + turn3[c, i]
        o_gmod[i] = -sens[i] / (mod[i] * mod[i])
        return carry

    lax.fori_loop(0, NPL, finish, 0)
    last = [
        pltpu.make_async_copy(o_gdisp, gdisp_h, store_sem.at[5]),
        pltpu.make_async_copy(o_gmod, gmod_h, store_sem.at[6]),
    ]
    for copy in last:
        copy.start()
    for copy in moved_out + outs + last:
        copy.wait()


def shards(
    displacement, velocity, modulus, classes, bond_integrity, densities, adjoint_disp, adjoint_vel
):
    block = (NPL, NROW, NLANE)
    field = (3,) + block
    shape = jax.ShapeDtypeStruct
    vmem = pltpu.VMEM
    anywhere = pl.BlockSpec(memory_space=pl.ANY)
    scratch = [
        vmem(field, F32),
        vmem(field, F32),
        vmem(block, F32),
        vmem(block, jnp.int32),
        vmem((32,) + block, F32),
        vmem(field, F32),
        vmem(field, F32),
        vmem(block, F32),
        vmem((SETS * 11, 12, 32, NLANE), F32),
        vmem((5, 12, 32, NLANE), F32),
        vmem((32,) + block, F32),
        vmem((32,) + block, F32),
        vmem((32,) + block, F32),
        vmem((32,) + block, F32),
        vmem((4, 22, NROW, NLANE), F32),
        vmem(field, F32),
        vmem(field, F32),
        vmem(field, F32),
        vmem(field, F32),
        vmem(block, F32),
        vmem(field, F32),
        vmem(field, F32),
        vmem(field, F32),
        vmem(block, F32),
        vmem((SETS, NROW, NLANE), F32),
        vmem((SETS, NPL, 8, NLANE), F32),
        vmem((2, SETS, 2, NLANE), F32),
        vmem((2, SETS, 6, NROW, NLANE), F32),
        vmem((2, SETS, NROW, NLANE), F32),
        vmem((2, SETS, 1, NLANE), F32),
        vmem((SETS, NPL, 8, NLANE), F32),
        vmem((2, SETS, 6, NROW, NLANE), F32),
        vmem((2, SETS, 8, NLANE), F32),
        vmem((2, 2, SETS, 2, NLANE), F32),
        vmem((2, 2, SETS, 1, NLANE), F32),
        pltpu.SemaphoreType.DMA((7,)),
        pltpu.SemaphoreType.DMA((7,)),
        pltpu.SemaphoreType.DMA((53,)),
        pltpu.SemaphoreType.DMA((53,)),
    ]
    return pl.pallas_call(
        kernel,
        out_shape=(
            shape(field, F32),
            shape(field, F32),
            shape(field, F32),
            shape(field, F32),
            shape(block, F32),
        ),
        in_specs=[anywhere] * 5 + [pl.BlockSpec(memory_space=pltpu.SMEM)] + [anywhere] * 2,
        out_specs=[anywhere] * 5,
        scratch_shapes=scratch,
        compiler_params=pltpu.CompilerParams(
            collective_id=0, has_side_effects=True, vmem_limit_bytes=48 * 1024 * 1024
        ),
        name="rock_wall_step",
    )(
        displacement,
        velocity,
        modulus,
        classes,
        bond_integrity,
        densities,
        adjoint_disp,
        adjoint_vel,
    )


def solution(mesh):
    field = P(None, "rad", "dep", "az")
    block = P("rad", "dep", "az")
    return jax.shard_map(
        shards,
        mesh=mesh,
        in_specs=(field, field, block, block, field, P(), field, field),
        out_specs=(field, field, field, field, block),
        check_vma=False,
    )
```

```python
import math

import jax
import jax.numpy as jnp
from jax import lax
from jax.experimental import pallas as pl
from jax.experimental.pallas import tpu as pltpu
from jax.sharding import PartitionSpec as P

BOND_OFFSETS = [
    (p, q, r)
    for p in range(-2, 3)
    for q in range(-2, 3)
    for r in range(-2, 3)
    if 0 < p * p + q * q + r * r <= 4
]
F32 = jnp.float32
NPL, NROW, NLANE = 8, 16, 128
DISP, CARRIED, MOVED, BACK = range(4)
SETS = 4
MESH = pl.DeviceIdType.MESH
NEIGHBOURS = [
    (da, dr, dd)
    for dd in (0, 1)
    for dr in (-1, 0, 1)
    for da in (-1, 0, 1)
    if (da, dr, dd) != (0, 0, 0)
]
MESSAGES = sorted(NEIGHBOURS, key=lambda n: (not (n[0] == 0 and n[2] == 0), abs(n[1])))
NEAR = [n for n in MESSAGES if n[1] == 0]
RADIAL = {
    side: [n for n in MESSAGES if n[1] == (-1 if side else 1)] for side in (0, 1)
}


def size_of(offset):
    length_sq = sum(o * o for o in offset)
    mult = max(abs(o) for o in offset)
    return mult, 2.0 * mult / length_sq, mult / math.sqrt(length_sq)


def signed(offset, parts):
    total = None
    for o, part in zip(offset, parts):
        if o != 0:
            if total is None:
                total = part if o > 0 else -part
            else:
                total = total + part if o > 0 else total - part
    return total


def add_signed(offset, parts, value):
    return [
        part if o == 0 else (part + value if o > 0 else part - value)
        for o, part in zip(offset, parts)
    ]


def kernel(
    disp_h,
    vel_h,
    mod_h,
    cls_h,
    bi_h,
    dens,
    adjd_h,
    adjv_h,
    moved_h,
    newv_h,
    gdisp_h,
    gvel_h,
    gmod_h,
    disp,
    vel,
    mod,
    cls,
    bi,
    adjd,
    adjv,
    rden,
    w,
    m,
    ecoef,
    gcoef,
    acoef,
    bcoef,
    xcoef,
    force1,
    force2,
    turn2,
    turn3,
    sens,
    o_newv,
    o_gvel,
    o_gdisp,
    o_gmod,
    pack,
    sd,
    se,
    sf,
    rp,
    rpr,
    rd,
    rf,
    rdr,
    re,
    rer,
    load_sem,
    store_sem,
    send_sem,
    recv_sem,
):
    az, rad, dep = lax.axis_index("az"), lax.axis_index("rad"), lax.axis_index("dep")
    naz, nrad = lax.axis_size("az"), lax.axis_size("rad")
    lane = lax.broadcasted_iota(jnp.int32, (NROW, NLANE), 1)
    lane_all = lax.broadcasted_iota(jnp.int32, (NPL, NROW, NLANE), 2)
    lane8_all = lax.broadcasted_iota(jnp.int32, (NPL, 8, NLANE), 2)
    lane8 = lax.broadcasted_iota(jnp.int32, (8, NLANE), 1)
    sub8 = lax.broadcasted_iota(jnp.int32, (8, NLANE), 0)

    def place(n):
        da, dr, dd = n
        return {
            "az": lax.rem(az + (da + naz), naz),
            "rad": lax.rem(rad + (dr + nrad), nrad),
            "dep": (1 - dep) if dd else dep,
        }

    barrier = pltpu.get_barrier_semaphore()
    for n in NEIGHBOURS:
        pl.semaphore_signal(barrier, inc=1, device_id=place(n), device_id_type=MESH)

    loads = {}
    for j, (name, src, dst) in enumerate(
        (
            ("disp", disp_h, disp),
            ("mod", mod_h, mod),
            ("cls", cls_h, cls),
            ("adjv", adjv_h, adjv),
            ("bi", bi_h, bi),
            ("vel", vel_h, vel),
            ("adjd", adjd_h, adjd),
        )
    ):
        loads[name] = pltpu.make_async_copy(src, dst, load_sem.at[j])
        loads[name].start()

    edge_row = 15 - 15 * dep
    second_row = 14 - 13 * dep
    halo_row = 8 + 16 - 17 * dep
    halo_row2 = 8 + 17 - 19 * dep
    blank = pl.multiple_of(24 * dep, 8)

    def clear(ref):
        ref[:, pl.ds(blank, 8), :] = jnp.zeros((12, 8, NLANE), F32)
        for plane in (0, 1, 10, 11):
            ref[plane] = jnp.zeros((32, NLANE), F32)

    def clear_w(j, carry):
        clear(w.at[j])
        return carry

    def clear_m(j, carry):
        clear(m.at[j])
        return carry

    lax.fori_loop(0, SETS * 9, clear_w, 0)
    lax.fori_loop(0, 5, clear_m, 0)
    sd[...] = jnp.zeros(sd.shape, F32)
    pack[...] = jnp.zeros(pack.shape, F32)

    def chan(t, c, r):
        return w.at[t * 9 + c * 3 + 1 + r]

    def near(t, c, offset, i):
        p, q, r = offset
        if abs(r) == 2:
            return w[SETS * 9 + t * 2 + (r > 0), i + 2, 8:24, :]
        return w[t * 9 + c * 3 + 1 + r, i + (2 + p), 8 + q : 24 + q, :]

    def near_m(offset, i):
        p, q, r = offset
        return m[2 + r, i + (2 + p), 8 + q : 24 + q, :]

    def centre(t, i):
        return [w[t * 9 + c * 3 + 1, i + 2, 8:24, :] for c in range(3)]

    def project(t, offset, i, cen):
        parts = [near(t, c, offset, i) if offset[c] else None for c in range(3)]
        return signed(offset, parts) - signed(offset, cen)

    def pack_planes(t, first, count, with_mod):
        at = pl.ds(2 + first, count)
        here = pl.ds(first, count)
        groups = None
        lanes = lane_all[:count]
        for c in range(4 if with_mod else 3):
            ref = m.at[2] if c == 3 else chan(t, c, 0)
            rolled = pltpu.roll(ref[at, 8:24, :], 4 * c + 2, 2)
            groups = rolled if c == 0 else jnp.where(lanes >= 4 * c, rolled, groups)
            sd[t, here, c : c + 1, :] = ref[at, pl.ds(8 + edge_row, 1), :]
            if c in (1, 3):
                row = 4 if c == 1 else 5
                sd[t, here, row : row + 1, :] = ref[at, pl.ds(8 + second_row, 1), :]
        packed = pack[t]
        for j in range(count):
            i = first + j
            rolled = pltpu.roll(groups[j], 16 * i, 1) if i else groups[j]
            packed = jnp.where(lane // 16 == i, rolled, packed)
        pack[t] = packed

    def pack_faces(t, with_mod):
        for side in (0, 1):
            outer, inner = (9, 8) if side else (2, 3)
            for c in range(3):
                sf[side, t, c] = chan(t, c, 0)[outer, 8:24, :]
            sf[side, t, 3] = chan(t, 0, 0)[inner, 8:24, :]
            if with_mod:
                sf[side, t, 4] = m[2, outer, 8:24, :]
                sf[side, t, 5] = m[2, inner, 8:24, :]

    def pack_corners(t):
        packed = pack[t]
        for side in (0, 1):
            turned = pltpu.roll(packed, 16, 1) if side else packed
            for half in (0, 1):
                y = jnp.where(lane8 < 16, turned[8 * half : 8 * half + 8], 0.0)
                for bit in (1, 2, 4):
                    y = jnp.where((sub8 & bit) != 0, pltpu.roll(y, 16 * bit, 1), y)
                se[side, t, half : half + 1, :] = jnp.sum(y, axis=0, keepdims=True)

    def copies(phase):
        made = {}
        first, count = ((0, 2), (2, 1), (3, 1))[phase]
        sets = pl.ds(first, count)
        for j, n in enumerate(MESSAGES):
            da, dr, dd = n
            a = 0 if da == 1 else 1
            out = 1 if dr == 1 else 0
            r = 1 - out
            if da == 0 and dd == 0:
                planes = pl.ds(0, 6 if phase == 0 else 4)
                pair = sf.at[out, first, planes], rf.at[r, first, planes]
            elif da == 0 and dr == 0:
                pair = sd.at[sets], rd.at[sets]
            elif da == 0:
                plane = 7 if dr == 1 else 0
                rows = pl.ds(0, 4)
                pair = sd.at[sets, plane, rows], rdr.at[r, sets, rows]
            elif dr == 0 and dd == 0:
                pair = pack.at[sets], rp.at[a, sets]
            elif dr == 0:
                pair = pack.at[sets, pl.ds(edge_row, 1)], rpr.at[a, sets]
            elif dd == 0:
                pair = se.at[out, sets], re.at[a, r, sets]
            else:
                pair = se.at[out, sets, pl.ds(1 - dep, 1)], rer.at[a, r, sets]
            made[n] = pltpu.make_async_remote_copy(
                src_ref=pair[0],
                dst_ref=pair[1],
                send_sem=send_sem.at[phase * 17 + j],
                recv_sem=recv_sem.at[phase * 17 + j],
                device_id=place(n),
                device_id_type=MESH,
            )
        return made

    def carried_copies():
        made = {}
        for out in (0, 1):
            made[1 - out] = pltpu.make_async_remote_copy(
                src_ref=sf.at[out, CARRIED, pl.ds(0, 4)],
                dst_ref=rf.at[1 - out, CARRIED, pl.ds(0, 4)],
                send_sem=send_sem.at[51 + out],
                recv_sem=recv_sem.at[51 + out],
                device_id=place((0, 1 if out else -1, 0)),
                device_id_type=MESH,
            )
        return made

    def both(left, right, lanes):
        return jnp.where(lanes % 4 < 2, left, right)

    def shifted(value, edge, lanes, by):
        last = value.ndim - 1
        if by > 0:
            return pltpu.roll(jnp.where(lanes < by, edge, value), NLANE - by, last)
        return pltpu.roll(jnp.where(lanes >= NLANE + by, edge, value), -by, last)

    def spread(row, step, bits):
        y = jnp.broadcast_to(row, (8, NLANE))
        for bit in bits:
            turned = pltpu.roll(y, (NLANE - step * bit) % NLANE, 1)
            y = jnp.where((sub8 & bit) != 0, turned, y)
        return y

    def turn_left(value, by):
        return pltpu.roll(value, lax.rem(2 * NLANE - by, NLANE), 1)

    def take_own(t, with_mod):
        sides = both(rp[0, t], rp[1, t], lane)
        sides = jnp.stack(
            [pltpu.roll(sides, NLANE - 16 * i, 1) if i else sides for i in range(NPL)]
        )
        rows = spread(both(rpr[0, t], rpr[1, t], lane8[0:1]), 4, (1, 2))
        rows = jnp.stack([pltpu.roll(rows, NLANE - 16 * i - 2, 1) for i in range(NPL)])
        tile = rd[t]
        own = pl.ds(2, NPL)
        for c in range(4 if with_mod else 3):
            ref = m.at[2] if c == 3 else chan(t, c, 0)
            value = ref[own, 8:24, :]
            edge = pltpu.roll(sides, NLANE - (4 * c + 2), 2)
            for r in (-2, -1, 1, 2) if c >= 2 else (-1, 1):
                if c == 3:
                    to = m.at[2 + r]
                elif abs(r) == 2:
                    to = w.at[SETS * 9 + t * 2 + (r > 0)]
                else:
                    to = chan(t, c, r)
                to[own, 8:24, :] = shifted(value, edge, lane_all, r)
        for r in (-1, 0, 1):
            moved = tile if r == 0 else shifted(tile, rows, lane8_all, r)
            for c in range(4 if with_mod else 3):
                to = m.at[2 + r] if c == 3 else chan(t, c, r)
                to[own, pl.ds(halo_row, 1), :] = moved[:, c : c + 1]
        chan(t, 1, 0)[own, pl.ds(halo_row2, 1), :] = tile[:, 4:5]
        if with_mod:
            m[2, own, pl.ds(halo_row2, 1), :] = tile[:, 5:6]

    def take_radial(t, side, with_mod):
        at, far = (10, 11) if side else (1, 0)
        there = (rad < nrad - 1) if side else (rad > 0)
        present = jnp.where(there, 1.0, 0.0).astype(F32)
        edges = [
            spread(
                both(
                    re[0, side, t, h : h + 1, :], re[1, side, t, h : h + 1, :], lane8[0:1]
                ),
                16,
                (1, 2, 4),
            )
            for h in (0, 1)
        ]
        for c in range(4 if with_mod else 3):
            value = rf[side, t, 4 if c == 3 else c]
            turned = [pltpu.roll(e, NLANE - (4 * c + 2), 1) for e in edges]
            edge = jnp.concatenate(turned, axis=0)
            for r in (-1, 0, 1):
                new = value if r == 0 else shifted(value, edge, lane, r)
                if c == 3:
                    m[2 + r, at, 8:24, :] = new * present
                else:
                    chan(t, c, r)[at, 8:24, :] = new
        chan(t, 0, 0)[far, 8:24, :] = rf[side, t, 3]
        if with_mod:
            m[2, far, 8:24, :] = rf[side, t, 5] * present
        rows = spread(both(rer[0, side, t], rer[1, side, t], lane8[0:1]), 4, (1, 2))
        edge = turn_left(rows, 16 * 7 * dep + 2)
        tile = rdr[side, t]
        for r in (-1, 0, 1):
            moved = tile if r == 0 else shifted(tile, edge, lane8, r)
            for c in range(4 if with_mod else 3):
                if c == 3:
                    m[2 + r, at, pl.ds(halo_row, 1), :] = moved[3:4] * present
                else:
                    chan(t, c, r)[at, pl.ds(halo_row, 1), :] = moved[c : c + 1]

    def bond_first(offset, i, cen, cm, intact, forces):
        mult, kappa, scale = size_of(offset)
        nm = near_m(offset, i)
        half = cm * nm / (cm + nm)
        e = intact * half * scale
        bend = jnp.tanh(kappa * project(DISP, offset, i, cen))
        push = e * bend
        g = e * half
        return add_signed(offset, forces, push), (
            e,
            g,
            kappa * (e - push * bend),
            g * bend,
        )

    def bond_second(offset, i, cen, cen_z, e, g, forces, turns, total):
        kappa = size_of(offset)[1]
        bend = jnp.tanh(kappa * project(MOVED, offset, i, cen))
        pull = project(CARRIED, offset, i, cen_z)
        push = e * bend
        stiff = kappa * (e - push * bend) * pull
        forces = add_signed(offset, forces, push)
        turns = add_signed(offset, turns, stiff)
        return forces, turns, total + g * bend * pull

    def bond_third(offset, i, cen_z, a, b, turns, total):
        pull = project(BACK, offset, i, cen_z)
        return add_signed(offset, turns, a * pull), total + b * pull

    def zeros(count):
        return [jnp.zeros((NROW, NLANE), F32) for _ in range(count)]

    def crossing(side):
        sign = 1 if side else -1
        outer, inner = (7, 6) if side else (0, 1)
        found = [(outer, k) for k, o in enumerate(BOND_OFFSETS) if o[0] == sign]
        double = BOND_OFFSETS.index((2 * sign, 0, 0))
        return found + [(outer, double), (inner, double)]

    def cross_first(side):
        for j, (i, k) in enumerate(crossing(side)):
            offset = BOND_OFFSETS[k]
            forces = [force1[c, i] for c in range(3)]
            forces, made = bond_first(
                offset, i, centre(DISP, i), m[2, i + 2, 8:24, :], bi[k, i], forces
            )
            for c in range(3):
                if offset[c]:
                    force1[c, i] = forces[c]
            for n, value in enumerate(made):
                xcoef[n, side * 11 + j] = value

    def cross_second(side):
        for j, (i, k) in enumerate(crossing(side)):
            offset = BOND_OFFSETS[k]
            x = side * 11 + j
            forces, turns, total = bond_second(
                offset,
                i,
                centre(MOVED, i),
                centre(CARRIED, i),
                xcoef[0, x],
                xcoef[1, x],
                [force2[c, i] for c in range(3)],
                [turn2[c, i] for c in range(3)],
                sens[i],
            )
            for c in range(3):
                if offset[c]:
                    force2[c, i] = forces[c]
                    turn2[c, i] = turns[c]
            sens[i] = total

    def cross_third(side):
        for j, (i, k) in enumerate(crossing(side)):
            offset = BOND_OFFSETS[k]
            x = side * 11 + j
            turns, total = bond_third(
                offset,
                i,
                centre(BACK, i),
                xcoef[2, x],
                xcoef[3, x],
                [turn3[c, i] for c in range(3)],
                sens[i],
            )
            for c in range(3):
                if offset[c]:
                    turn3[c, i] = turns[c]
            sens[i] = total

    own = pl.ds(2, NPL)
    sent = copies(0)
    sent_carried = carried_copies()
    loads["disp"].wait()
    loads["mod"].wait()
    m[2, own, 8:24, :] = mod[...]
    for c in range(3):
        chan(DISP, c, 0)[own, 8:24, :] = disp[c]
    pack_faces(DISP, True)
    pl.semaphore_wait(barrier, len(NEIGHBOURS))
    for n in MESSAGES[:2]:
        sent[n].start()
    loads["cls"].wait()
    loads["adjv"].wait()
    kinds = cls[...]
    density = jnp.full((NPL, NROW, NLANE), dens[0])
    for level in range(1, 8):
        density = jnp.where(kinds == level, dens[level], density)
    rden[...] = 1.0 / density
    for c in range(3):
        chan(CARRIED, c, 0)[own, 8:24, :] = 0.25 * adjv[c] * rden[...]
    pack_planes(DISP, 0, NPL, True)
    pack_planes(CARRIED, 0, NPL, False)
    pack_corners(DISP)
    pack_corners(CARRIED)
    pack_faces(CARRIED, False)
    for n in MESSAGES[2:]:
        sent[n].start()
    for side in (0, 1):
        sent_carried[side].start()
    for name in ("bi", "vel", "adjd"):
        loads[name].wait()
    for n in NEAR:
        sent[n].wait_recv()
    take_own(DISP, True)
    take_own(CARRIED, False)

    def sweep_first(i, carry):
        cen, cm, forces = centre(DISP, i), m[2, i + 2, 8:24, :], zeros(3)
        for k, offset in enumerate(BOND_OFFSETS):
            forces, made = bond_first(offset, i, cen, cm, bi[k, i], forces)
            for ref, value in zip((ecoef, gcoef, acoef, bcoef), made):
                ref[k, i] = value
        for c in range(3):
            force1[c, i] = forces[c]
        return carry

    lax.fori_loop(0, NPL, sweep_first, 0)

    def end_first(first, count):
        here = pl.ds(first, count)
        for c in range(3):
            accel = force1[c, here] * rden[here]
            moved = disp[c, here] + 0.5 * vel[c, here] + 0.125 * accel
            chan(MOVED, c, 0)[pl.ds(2 + first, count), 8:24, :] = moved
        pack_planes(MOVED, first, count, False)

    end_first(2, 4)
    for n in MESSAGES:
        sent[n].wait_send()
    for side in (0, 1):
        for n in RADIAL[side]:
            sent[n].wait_recv()
        take_radial(DISP, side, True)
        cross_first(side)
    end_first(0, 2)
    end_first(6, 2)
    pack_faces(MOVED, False)
    pack_corners(MOVED)

    sent = copies(1)
    for n in MESSAGES:
        sent[n].start()
    moved_out = [
        pltpu.make_async_copy(
            chan(MOVED, c, 0).at[pl.ds(2, NPL), pl.ds(8, NROW)], moved_h.at[c], store_sem.at[c]
        )
        for c in range(3)
    ]
    for copy in moved_out:
        copy.start()
    for side in (0, 1):
        sent_carried[side].wait_recv()
        sent_carried[side].wait_send()
        take_radial(CARRIED, side, False)
    for n in NEAR:
        sent[n].wait_recv()
    take_own(MOVED, False)

    def sweep_second(i, carry):
        cen, cen_z = centre(MOVED, i), centre(CARRIED, i)
        forces, turns, total = zeros(3), zeros(3), zeros(1)[0]
        for k, offset in enumerate(BOND_OFFSETS):
            forces, turns, total = bond_second(
                offset, i, cen, cen_z, ecoef[k, i], gcoef[k, i], forces, turns, total
            )
        for c in range(3):
            force2[c, i] = forces[c]
            turn2[c, i] = turns[c]
        sens[i] = total
        return carry

    lax.fori_loop(0, NPL, sweep_second, 0)

    def end_second(first, count):
        here = pl.ds(first, count)
        for c in range(3):
            total = adjd[c, here] + turn2[c, here]
            turn2[c, here] = total
            back = (0.25 * adjv[c, here] + 0.125 * total) * rden[here]
            chan(BACK, c, 0)[pl.ds(2 + first, count), 8:24, :] = back
        pack_planes(BACK, first, count, False)

    end_second(2, 4)
    for n in MESSAGES:
        sent[n].wait_send()
    for side in (0, 1):
        for n in RADIAL[side]:
            sent[n].wait_recv()
        take_radial(MOVED, side, False)
        cross_second(side)
    end_second(0, 2)
    end_second(6, 2)
    pack_faces(BACK, False)
    pack_corners(BACK)

    sent = copies(2)
    for n in MESSAGES:
        sent[n].start()

    for c in range(3):
        accel = (force1[c] + force2[c]) * rden[...]
        o_newv[c] = vel[c] + 0.25 * accel
        o_gvel[c] = adjv[c] + 0.5 * turn2[c]
    outs = [
        pltpu.make_async_copy(o_newv, newv_h, store_sem.at[3]),
        pltpu.make_async_copy(o_gvel, gvel_h, store_sem.at[4]),
    ]
    for copy in outs:
        copy.start()
    for n in NEAR:
        sent[n].wait_recv()
    take_own(BACK, False)

    def sweep_third(i, carry):
        cen_z, turns, total = centre(BACK, i), zeros(3), sens[i]
        for k, offset in enumerate(BOND_OFFSETS):
            turns, total = bond_third(offset, i, cen_z, acoef[k, i], bcoef[k, i], turns, total)
        for c in range(3):
            turn3[c, i] = turns[c]
        sens[i] = total
        return carry

    lax.fori_loop(0, NPL, sweep_third, 0)
    for n in MESSAGES:
        sent[n].wait_send()
    for side in (0, 1):
        for n in RADIAL[side]:
            sent[n].wait_recv()
        take_radial(BACK, side, False)
        cross_third(side)

    for c in range(3):
        o_gdisp[c] = turn2[c] + turn3[c]
    o_gmod[...] = -sens[...] / (mod[...] * mod[...])
    last = [
        pltpu.make_async_copy(o_gdisp, gdisp_h, store_sem.at[5]),
        pltpu.make_async_copy(o_gmod, gmod_h, store_sem.at[6]),
    ]
    for copy in last:
        copy.start()
    for copy in moved_out + outs + last:
        copy.wait()


def shards(
    displacement, velocity, modulus, classes, bond_integrity, densities, adjoint_disp, adjoint_vel
):
    block = (NPL, NROW, NLANE)
    field = (3,) + block
    shape = jax.ShapeDtypeStruct
    vmem = pltpu.VMEM
    anywhere = pl.BlockSpec(memory_space=pl.ANY)
    scratch = [
        vmem(field, F32),
        vmem(field, F32),
        vmem(block, F32),
        vmem(block, jnp.int32),
        vmem((32,) + block, F32),
        vmem(field, F32),
        vmem(field, F32),
        vmem(block, F32),
        vmem((SETS * 11, 12, 32, NLANE), F32),
        vmem((5, 12, 32, NLANE), F32),
        vmem((32,) + block, F32),
        vmem((32,) + block, F32),
        vmem((32,) + block, F32),
        vmem((32,) + block, F32),
        vmem((4, 22, NROW, NLANE), F32),
        vmem(field, F32),
        vmem(field, F32),
        vmem(field, F32),
        vmem(field, F32),
        vmem(block, F32),
        vmem(field, F32),
        vmem(field, F32),
        vmem(field, F32),
        vmem(block, F32),
        vmem((SETS, NROW, NLANE), F32),
        vmem((SETS, NPL, 8, NLANE), F32),
        vmem((2, SETS, 2, NLANE), F32),
        vmem((2, SETS, 6, NROW, NLANE), F32),
        vmem((2, SETS, NROW, NLANE), F32),
        vmem((2, SETS, 1, NLANE), F32),
        vmem((SETS, NPL, 8, NLANE), F32),
        vmem((2, SETS, 6, NROW, NLANE), F32),
        vmem((2, SETS, 8, NLANE), F32),
        vmem((2, 2, SETS, 2, NLANE), F32),
        vmem((2, 2, SETS, 1, NLANE), F32),
        pltpu.SemaphoreType.DMA((7,)),
        pltpu.SemaphoreType.DMA((7,)),
        pltpu.SemaphoreType.DMA((53,)),
        pltpu.SemaphoreType.DMA((53,)),
    ]
    made = pl.pallas_call(
        kernel,
        out_shape=(
            shape(field, F32),
            shape(field, F32),
            shape(field, F32),
            shape(field, F32),
            shape(block, F32),
        ),
        in_specs=[anywhere] * 5 + [pl.BlockSpec(memory_space=pltpu.SMEM)] + [anywhere] * 2,
        out_specs=[anywhere] * 5,
        scratch_shapes=scratch,
        compiler_params=pltpu.CompilerParams(
            collective_id=0, has_side_effects=True, vmem_limit_bytes=62 * 1024 * 1024
        ),
        name="rock_wall_step",
    )(
        displacement,
        velocity,
        modulus,
        classes,
        bond_integrity,
        densities,
        adjoint_disp,
        adjoint_vel,
    )
    return pl.pallas_call(
        hand_over,
        out_shape=tuple(shape(x.shape, F32) for x in made),
        in_specs=[anywhere] * 5,
        out_specs=[anywhere] * 5,
        scratch_shapes=[pltpu.SemaphoreType.DMA((5,))],
        name="hand_over",
    )(*made)


def hand_over(*refs):
    copies = [pltpu.make_async_copy(refs[j], refs[5 + j], refs[10].at[j]) for j in range(5)]
    for copy in copies:
        copy.start()
    for copy in copies:
        copy.wait()


def solution(mesh):
    field = P(None, "rad", "dep", "az")
    block = P("rad", "dep", "az")
    return jax.shard_map(
        shards,
        mesh=mesh,
        in_specs=(field, field, block, block, field, P(), field, field),
        out_specs=(field, field, field, field, block),
        check_vma=False,
    )
```

```python
import math

import jax
import jax.numpy as jnp
from jax import lax
from jax.experimental import pallas as pl
from jax.experimental.pallas import tpu as pltpu
from jax.sharding import PartitionSpec as P

BOND_OFFSETS = [
    (p, q, r)
    for p in range(-2, 3)
    for q in range(-2, 3)
    for r in range(-2, 3)
    if 0 < p * p + q * q + r * r <= 4
]
F32 = jnp.float32
NPL, NROW, NLANE = 8, 16, 128
DISP, CARRIED, MOVED, BACK = range(4)
SETS = 4
MESH = pl.DeviceIdType.MESH
NEIGHBOURS = [
    (da, dr, dd)
    for dd in (0, 1)
    for dr in (-1, 0, 1)
    for da in (-1, 0, 1)
    if (da, dr, dd) != (0, 0, 0)
]
MESSAGES = sorted(NEIGHBOURS, key=lambda n: (abs(n[1]), n[2] if n[1] else 0, abs(n[0])))
PARTNER = (0, 0, 1)
NEAR = [n for n in MESSAGES if n[1] == 0 and n != PARTNER]
ALONG = [k for k, o in enumerate(BOND_OFFSETS) if o[2] == 0]
ACROSS = [k for k, o in enumerate(BOND_OFFSETS) if o[2] != 0]
RADIAL = {
    side: [n for n in MESSAGES if n[1] == (-1 if side else 1)] for side in (0, 1)
}


def size_of(offset):
    length_sq = sum(o * o for o in offset)
    mult = max(abs(o) for o in offset)
    return mult, 2.0 * mult / length_sq, mult / math.sqrt(length_sq)


def signed(offset, parts):
    total = None
    for o, part in zip(offset, parts):
        if o != 0:
            if total is None:
                total = part if o > 0 else -part
            else:
                total = total + part if o > 0 else total - part
    return total


def add_signed(offset, parts, value):
    return [
        part if o == 0 else (part + value if o > 0 else part - value)
        for o, part in zip(offset, parts)
    ]


def kernel(
    disp_h,
    vel_h,
    mod_h,
    cls_h,
    bi_h,
    dens,
    adjd_h,
    adjv_h,
    moved_h,
    newv_h,
    gdisp_h,
    gvel_h,
    gmod_h,
    disp,
    vel,
    mod,
    cls,
    bi,
    adjd,
    adjv,
    rden,
    w,
    m,
    ecoef,
    gcoef,
    acoef,
    bcoef,
    xcoef,
    force1,
    force2,
    turn2,
    turn3,
    sens,
    o_newv,
    o_gvel,
    o_gdisp,
    o_gmod,
    pack,
    sd,
    se,
    sf,
    rp,
    rpr,
    rd,
    rf,
    rdr,
    re,
    rer,
    load_sem,
    store_sem,
    send_sem,
    recv_sem,
):
    az, rad, dep = lax.axis_index("az"), lax.axis_index("rad"), lax.axis_index("dep")
    naz, nrad = lax.axis_size("az"), lax.axis_size("rad")
    lane = lax.broadcasted_iota(jnp.int32, (NROW, NLANE), 1)
    lane_all = lax.broadcasted_iota(jnp.int32, (NPL, NROW, NLANE), 2)
    lane8_all = lax.broadcasted_iota(jnp.int32, (NPL, 8, NLANE), 2)
    lane8 = lax.broadcasted_iota(jnp.int32, (8, NLANE), 1)
    sub8 = lax.broadcasted_iota(jnp.int32, (8, NLANE), 0)

    def place(n):
        da, dr, dd = n
        return {
            "az": lax.rem(az + (da + naz), naz),
            "rad": lax.rem(rad + (dr + nrad), nrad),
            "dep": (1 - dep) if dd else dep,
        }

    barrier = pltpu.get_barrier_semaphore()
    for n in NEIGHBOURS:
        pl.semaphore_signal(barrier, inc=1, device_id=place(n), device_id_type=MESH)

    loads = {}
    for j, (name, src, dst) in enumerate(
        (
            ("disp", disp_h, disp),
            ("mod", mod_h, mod),
            ("cls", cls_h, cls),
            ("adjv", adjv_h, adjv),
            ("bi", bi_h, bi),
            ("vel", vel_h, vel),
            ("adjd", adjd_h, adjd),
        )
    ):
        loads[name] = pltpu.make_async_copy(src, dst, load_sem.at[j])
        loads[name].start()

    edge_row = 15 - 15 * dep
    second_row = 14 - 13 * dep
    halo_row = 8 + 16 - 17 * dep
    halo_row2 = 8 + 17 - 19 * dep
    blank = pl.multiple_of(24 * dep, 8)

    def clear(ref):
        ref[:, pl.ds(blank, 8), :] = jnp.zeros((12, 8, NLANE), F32)
        for plane in (0, 1, 10, 11):
            ref[plane] = jnp.zeros((32, NLANE), F32)

    def clear_w(j, carry):
        clear(w.at[j])
        return carry

    def clear_m(j, carry):
        clear(m.at[j])
        return carry

    lax.fori_loop(0, SETS * 9, clear_w, 0)
    lax.fori_loop(0, 5, clear_m, 0)
    sd[...] = jnp.zeros(sd.shape, F32)
    pack[...] = jnp.zeros(pack.shape, F32)

    def chan(t, c, r):
        return w.at[t * 9 + c * 3 + 1 + r]

    def near(t, c, offset, i):
        p, q, r = offset
        if abs(r) == 2:
            return w[SETS * 9 + t * 2 + (r > 0), i + 2, 8:24, :]
        return w[t * 9 + c * 3 + 1 + r, i + (2 + p), 8 + q : 24 + q, :]

    def near_m(offset, i):
        p, q, r = offset
        return m[2 + r, i + (2 + p), 8 + q : 24 + q, :]

    def centre(t, i):
        return [w[t * 9 + c * 3 + 1, i + 2, 8:24, :] for c in range(3)]

    def project(t, offset, i, cen):
        parts = [near(t, c, offset, i) if offset[c] else None for c in range(3)]
        return signed(offset, parts) - signed(offset, cen)

    own = pl.ds(2, NPL)

    def pack_planes(t, first, count, with_mod):
        at = pl.ds(2 + first, count)
        here = pl.ds(first, count)
        groups = None
        lanes = lane_all[:count]
        for c in range(4 if with_mod else 3):
            ref = m.at[2] if c == 3 else chan(t, c, 0)
            rolled = pltpu.roll(ref[at, 8:24, :], 4 * c + 2, 2)
            groups = rolled if c == 0 else jnp.where(lanes >= 4 * c, rolled, groups)
            sd[t, here, c : c + 1, :] = ref[at, pl.ds(8 + edge_row, 1), :]
            if c in (1, 3):
                row = 4 if c == 1 else 5
                sd[t, here, row : row + 1, :] = ref[at, pl.ds(8 + second_row, 1), :]
        packed = pack[t]
        for j in range(count):
            i = first + j
            rolled = pltpu.roll(groups[j], 16 * i, 1) if i else groups[j]
            packed = jnp.where(lane // 16 == i, rolled, packed)
        pack[t] = packed

    def pack_faces(t, with_mod):
        for side in (0, 1):
            outer, inner = (9, 8) if side else (2, 3)
            for c in range(3):
                sf[side, t, c] = chan(t, c, 0)[outer, 8:24, :]
            sf[side, t, 3] = chan(t, 0, 0)[inner, 8:24, :]
            if with_mod:
                sf[side, t, 4] = m[2, outer, 8:24, :]
                sf[side, t, 5] = m[2, inner, 8:24, :]

    def pack_corners(t):
        packed = pack[t]
        for side in (0, 1):
            turned = pltpu.roll(packed, 16, 1) if side else packed
            for half in (0, 1):
                y = jnp.where(lane8 < 16, turned[8 * half : 8 * half + 8], 0.0)
                for bit in (1, 2, 4):
                    y = jnp.where((sub8 & bit) != 0, pltpu.roll(y, 16 * bit, 1), y)
                se[side, t, half : half + 1, :] = jnp.sum(y, axis=0, keepdims=True)

    def copies(phase):
        made = {}
        first, count = ((0, 2), (2, 1), (3, 1))[phase]
        sets = pl.ds(first, count)
        for j, n in enumerate(MESSAGES):
            da, dr, dd = n
            a = 0 if da == 1 else 1
            out = 1 if dr == 1 else 0
            r = 1 - out
            if da == 0 and dd == 0:
                planes = pl.ds(0, 6 if phase == 0 else 4)
                pair = sf.at[out, first, planes], rf.at[r, first, planes]
            elif da == 0 and dr == 0:
                pair = sd.at[sets], rd.at[sets]
            elif da == 0:
                plane = 7 if dr == 1 else 0
                rows = pl.ds(0, 4)
                pair = sd.at[sets, plane, rows], rdr.at[r, sets, rows]
            elif dr == 0 and dd == 0:
                pair = pack.at[sets], rp.at[a, sets]
            elif dr == 0:
                pair = pack.at[sets, pl.ds(edge_row, 1)], rpr.at[a, sets]
            elif dd == 0:
                pair = se.at[out, sets], re.at[a, r, sets]
            else:
                pair = se.at[out, sets, pl.ds(1 - dep, 1)], rer.at[a, r, sets]
            made[n] = pltpu.make_async_remote_copy(
                src_ref=pair[0],
                dst_ref=pair[1],
                send_sem=send_sem.at[phase * 17 + j],
                recv_sem=recv_sem.at[phase * 17 + j],
                device_id=place(n),
                device_id_type=MESH,
            )
        return made

    def carried_copies():
        made = {}
        for out in (0, 1):
            made[1 - out] = pltpu.make_async_remote_copy(
                src_ref=sf.at[out, CARRIED, pl.ds(0, 4)],
                dst_ref=rf.at[1 - out, CARRIED, pl.ds(0, 4)],
                send_sem=send_sem.at[51 + out],
                recv_sem=recv_sem.at[51 + out],
                device_id=place((0, 1 if out else -1, 0)),
                device_id_type=MESH,
            )
        return made

    def both(left, right, lanes):
        return jnp.where(lanes % 4 < 2, left, right)

    def shifted(value, edge, lanes, by):
        last = value.ndim - 1
        if by > 0:
            return pltpu.roll(jnp.where(lanes < by, edge, value), NLANE - by, last)
        return pltpu.roll(jnp.where(lanes >= NLANE + by, edge, value), -by, last)

    def spread(row, step, bits):
        y = jnp.broadcast_to(row, (8, NLANE))
        for bit in bits:
            turned = pltpu.roll(y, (NLANE - step * bit) % NLANE, 1)
            y = jnp.where((sub8 & bit) != 0, turned, y)
        return y

    def turn_left(value, by):
        return pltpu.roll(value, lax.rem(2 * NLANE - by, NLANE), 1)

    def turned_arrays(t, with_mod):
        for c in range(4 if with_mod else 3):
            for r in (-2, -1, 1, 2) if c >= 2 else (-1, 1):
                if c == 3:
                    yield c, r, m.at[2 + r]
                elif abs(r) == 2:
                    yield c, r, w.at[SETS * 9 + t * 2 + (r > 0)]
                else:
                    yield c, r, chan(t, c, r)

    def take_partner(t, with_mod):
        tile = rd[t]
        for c in range(4 if with_mod else 3):
            to = m.at[2] if c == 3 else chan(t, c, 0)
            to[own, pl.ds(halo_row, 1), :] = tile[:, c : c + 1]
        chan(t, 1, 0)[own, pl.ds(halo_row2, 1), :] = tile[:, 4:5]
        if with_mod:
            m[2, own, pl.ds(halo_row2, 1), :] = tile[:, 5:6]
        for c, r, to in turned_arrays(t, with_mod):
            ref = m.at[2] if c == 3 else chan(t, c, 0)
            to[own, 8:24, :] = pltpu.roll(ref[own, 8:24, :], (NLANE - r) % NLANE, 2)

    def take_sides(t, with_mod):
        sides = both(rp[0, t], rp[1, t], lane)
        sides = jnp.stack(
            [pltpu.roll(sides, NLANE - 16 * i, 1) if i else sides for i in range(NPL)]
        )
        rows = spread(both(rpr[0, t], rpr[1, t], lane8[0:1]), 4, (1, 2))
        rows = jnp.stack([pltpu.roll(rows, NLANE - 16 * i - 2, 1) for i in range(NPL)])
        for c, r, to in turned_arrays(t, with_mod):
            edge = pltpu.roll(sides, (2 * NLANE - (4 * c + 2) - r) % NLANE, 2)
            lanes = lane_all >= NLANE - r if r > 0 else lane_all < -r
            to[own, 8:24, :] = jnp.where(lanes, edge, to[own, 8:24, :])
        tile = rd[t]
        for r in (-1, 1):
            moved = shifted(tile, rows, lane8_all, r)
            for c in range(4 if with_mod else 3):
                to = m.at[2 + r] if c == 3 else chan(t, c, r)
                to[own, pl.ds(halo_row, 1), :] = moved[:, c : c + 1]

    def take_radial(t, side, with_mod):
        at, far = (10, 11) if side else (1, 0)
        there = (rad < nrad - 1) if side else (rad > 0)
        present = jnp.where(there, 1.0, 0.0).astype(F32)
        edges = [
            spread(
                both(
                    re[0, side, t, h : h + 1, :], re[1, side, t, h : h + 1, :], lane8[0:1]
                ),
                16,
                (1, 2, 4),
            )
            for h in (0, 1)
        ]
        for c in range(4 if with_mod else 3):
            value = rf[side, t, 4 if c == 3 else c]
            turned = [pltpu.roll(e, NLANE - (4 * c + 2), 1) for e in edges]
            edge = jnp.concatenate(turned, axis=0)
            for r in (-1, 0, 1):
                new = value if r == 0 else shifted(value, edge, lane, r)
                if c == 3:
                    m[2 + r, at, 8:24, :] = new * present
                else:
                    chan(t, c, r)[at, 8:24, :] = new
        chan(t, 0, 0)[far, 8:24, :] = rf[side, t, 3]
        if with_mod:
            m[2, far, 8:24, :] = rf[side, t, 5] * present
        rows = spread(both(rer[0, side, t], rer[1, side, t], lane8[0:1]), 4, (1, 2))
        edge = turn_left(rows, 16 * 7 * dep + 2)
        tile = rdr[side, t]
        for r in (-1, 0, 1):
            moved = tile if r == 0 else shifted(tile, edge, lane8, r)
            for c in range(4 if with_mod else 3):
                if c == 3:
                    m[2 + r, at, pl.ds(halo_row, 1), :] = moved[3:4] * present
                else:
                    chan(t, c, r)[at, pl.ds(halo_row, 1), :] = moved[c : c + 1]

    def bond_first(offset, i, cen, cm, intact, forces):
        mult, kappa, scale = size_of(offset)
        nm = near_m(offset, i)
        half = cm * nm / (cm + nm)
        e = intact * half * scale
        bend = jnp.tanh(kappa * project(DISP, offset, i, cen))
        push = e * bend
        g = e * half
        return add_signed(offset, forces, push), (
            e,
            g,
            kappa * (e - push * bend),
            g * bend,
        )

    def bond_second(offset, i, cen, cen_z, e, g, forces, turns, total):
        kappa = size_of(offset)[1]
        bend = jnp.tanh(kappa * project(MOVED, offset, i, cen))
        pull = project(CARRIED, offset, i, cen_z)
        push = e * bend
        stiff = kappa * (e - push * bend) * pull
        forces = add_signed(offset, forces, push)
        turns = add_signed(offset, turns, stiff)
        return forces, turns, total + g * bend * pull

    def bond_third(offset, i, cen_z, a, b, turns, total):
        pull = project(BACK, offset, i, cen_z)
        return add_signed(offset, turns, a * pull), total + b * pull

    def zeros(count):
        return [jnp.zeros((NROW, NLANE), F32) for _ in range(count)]

    def crossing(side):
        sign = 1 if side else -1
        outer, inner = (7, 6) if side else (0, 1)
        found = [(outer, k) for k, o in enumerate(BOND_OFFSETS) if o[0] == sign]
        double = BOND_OFFSETS.index((2 * sign, 0, 0))
        return found + [(outer, double), (inner, double)]

    def cross_first(side):
        for j, (i, k) in enumerate(crossing(side)):
            offset = BOND_OFFSETS[k]
            forces = [force1[c, i] for c in range(3)]
            forces, made = bond_first(
                offset, i, centre(DISP, i), m[2, i + 2, 8:24, :], bi[k, i], forces
            )
            for c in range(3):
                if offset[c]:
                    force1[c, i] = forces[c]
            for n, value in enumerate(made):
                xcoef[n, side * 11 + j] = value

    def cross_second(side):
        for j, (i, k) in enumerate(crossing(side)):
            offset = BOND_OFFSETS[k]
            x = side * 11 + j
            forces, turns, total = bond_second(
                offset,
                i,
                centre(MOVED, i),
                centre(CARRIED, i),
                xcoef[0, x],
                xcoef[1, x],
                [force2[c, i] for c in range(3)],
                [turn2[c, i] for c in range(3)],
                sens[i],
            )
            for c in range(3):
                if offset[c]:
                    force2[c, i] = forces[c]
                    turn2[c, i] = turns[c]
            sens[i] = total

    def cross_third(side):
        for j, (i, k) in enumerate(crossing(side)):
            offset = BOND_OFFSETS[k]
            x = side * 11 + j
            turns, total = bond_third(
                offset,
                i,
                centre(BACK, i),
                xcoef[2, x],
                xcoef[3, x],
                [turn3[c, i] for c in range(3)],
                sens[i],
            )
            for c in range(3):
                if offset[c]:
                    turn3[c, i] = turns[c]
            sens[i] = total

    sent = copies(0)
    sent_carried = carried_copies()
    for name in ("disp", "mod", "cls", "adjv"):
        loads[name].wait()
    m[2, own, 8:24, :] = mod[...]
    for c in range(3):
        chan(DISP, c, 0)[own, 8:24, :] = disp[c]
    kinds = cls[...]
    density = jnp.full((NPL, NROW, NLANE), dens[0])
    for level in range(1, 8):
        density = jnp.where(kinds == level, dens[level], density)
    rden[...] = 1.0 / density
    for c in range(3):
        chan(CARRIED, c, 0)[own, 8:24, :] = 0.25 * adjv[c] * rden[...]
    for t in (DISP, CARRIED):
        pack_planes(t, 0, NPL, t == DISP)
        pack_faces(t, t == DISP)
        pack_corners(t)
    pl.semaphore_wait(barrier, len(NEIGHBOURS))
    for n in MESSAGES:
        sent[n].start()
    for side in (0, 1):
        sent_carried[side].start()
    for name in ("bi", "vel", "adjd"):
        loads[name].wait()

    def sweep_first(bonds, fresh):
        def plane(i, carry):
            cen, cm = centre(DISP, i), m[2, i + 2, 8:24, :]
            forces = zeros(3) if fresh else [force1[c, i] for c in range(3)]
            for k in bonds:
                forces, made = bond_first(BOND_OFFSETS[k], i, cen, cm, bi[k, i], forces)
                for ref, value in zip((ecoef, gcoef, acoef, bcoef), made):
                    ref[k, i] = value
            for c in range(3):
                force1[c, i] = forces[c]
            return carry

        lax.fori_loop(0, NPL, plane, 0)

    sent[PARTNER].wait_recv()
    take_partner(DISP, True)
    sweep_first(ALONG, True)
    for n in NEAR:
        sent[n].wait_recv()
    take_sides(DISP, True)
    sweep_first(ACROSS, False)

    def end_first(first, count):
        here = pl.ds(first, count)
        for c in range(3):
            accel = force1[c, here] * rden[here]
            moved = disp[c, here] + 0.5 * vel[c, here] + 0.125 * accel
            chan(MOVED, c, 0)[pl.ds(2 + first, count), 8:24, :] = moved
        pack_planes(MOVED, first, count, False)

    end_first(2, 4)
    for n in MESSAGES:
        sent[n].wait_send()
    for side in (0, 1):
        for n in RADIAL[side]:
            sent[n].wait_recv()
        take_radial(DISP, side, True)
        cross_first(side)
    end_first(0, 2)
    end_first(6, 2)
    pack_faces(MOVED, False)
    pack_corners(MOVED)

    sent = copies(1)
    for n in MESSAGES:
        sent[n].start()
    moved_out = [
        pltpu.make_async_copy(
            chan(MOVED, c, 0).at[pl.ds(2, NPL), pl.ds(8, NROW)], moved_h.at[c], store_sem.at[c]
        )
        for c in range(3)
    ]
    for copy in moved_out:
        copy.start()
    sent[PARTNER].wait_recv()
    take_partner(MOVED, False)
    take_partner(CARRIED, False)
    take_sides(CARRIED, False)
    for side in (0, 1):
        sent_carried[side].wait_recv()
        sent_carried[side].wait_send()
        take_radial(CARRIED, side, False)

    def sweep_second(bonds, fresh):
        def plane(i, carry):
            cen, cen_z = centre(MOVED, i), centre(CARRIED, i)
            if fresh:
                forces, turns, total = zeros(3), zeros(3), zeros(1)[0]
            else:
                forces = [force2[c, i] for c in range(3)]
                turns = [turn2[c, i] for c in range(3)]
                total = sens[i]
            for k in bonds:
                forces, turns, total = bond_second(
                    BOND_OFFSETS[k], i, cen, cen_z, ecoef[k, i], gcoef[k, i], forces, turns, total
                )
            for c in range(3):
                force2[c, i] = forces[c]
                turn2[c, i] = turns[c]
            sens[i] = total
            return carry

        lax.fori_loop(0, NPL, plane, 0)

    sweep_second(ALONG, True)
    for n in NEAR:
        sent[n].wait_recv()
    take_sides(MOVED, False)
    sweep_second(ACROSS, False)

    def end_second(first, count):
        here = pl.ds(first, count)
        for c in range(3):
            total = adjd[c, here] + turn2[c, here]
            turn2[c, here] = total
            back = (0.25 * adjv[c, here] + 0.125 * total) * rden[here]
            chan(BACK, c, 0)[pl.ds(2 + first, count), 8:24, :] = back
        pack_planes(BACK, first, count, False)

    end_second(2, 4)
    for n in MESSAGES:
        sent[n].wait_send()
    for side in (0, 1):
        for n in RADIAL[side]:
            sent[n].wait_recv()
        take_radial(MOVED, side, False)
        cross_second(side)
    end_second(0, 2)
    end_second(6, 2)
    pack_faces(BACK, False)
    pack_corners(BACK)

    sent = copies(2)
    for n in MESSAGES:
        sent[n].start()

    for c in range(3):
        accel = (force1[c] + force2[c]) * rden[...]
        o_newv[c] = vel[c] + 0.25 * accel
        o_gvel[c] = adjv[c] + 0.5 * turn2[c]
    outs = [
        pltpu.make_async_copy(o_newv, newv_h, store_sem.at[3]),
        pltpu.make_async_copy(o_gvel, gvel_h, store_sem.at[4]),
    ]
    for copy in outs:
        copy.start()
    def sweep_third(bonds, fresh):
        def plane(i, carry):
            cen_z, total = centre(BACK, i), sens[i]
            turns = zeros(3) if fresh else [turn3[c, i] for c in range(3)]
            for k in bonds:
                turns, total = bond_third(
                    BOND_OFFSETS[k], i, cen_z, acoef[k, i], bcoef[k, i], turns, total
                )
            for c in range(3):
                turn3[c, i] = turns[c]
            sens[i] = total
            return carry

        lax.fori_loop(0, NPL, plane, 0)

    sent[PARTNER].wait_recv()
    take_partner(BACK, False)
    sweep_third(ALONG, True)
    for n in NEAR:
        sent[n].wait_recv()
    take_sides(BACK, False)
    sweep_third(ACROSS, False)
    for n in MESSAGES:
        sent[n].wait_send()
    for side in (0, 1):
        for n in RADIAL[side]:
            sent[n].wait_recv()
        take_radial(BACK, side, False)
        cross_third(side)

    for c in range(3):
        o_gdisp[c] = turn2[c] + turn3[c]
    o_gmod[...] = -sens[...] / (mod[...] * mod[...])
    last = [
        pltpu.make_async_copy(o_gdisp, gdisp_h, store_sem.at[5]),
        pltpu.make_async_copy(o_gmod, gmod_h, store_sem.at[6]),
    ]
    for copy in last:
        copy.start()
    for copy in moved_out + outs + last:
        copy.wait()


def shards(
    displacement, velocity, modulus, classes, bond_integrity, densities, adjoint_disp, adjoint_vel
):
    block = (NPL, NROW, NLANE)
    field = (3,) + block
    shape = jax.ShapeDtypeStruct
    vmem = pltpu.VMEM
    anywhere = pl.BlockSpec(memory_space=pl.ANY)
    scratch = [
        vmem(field, F32),
        vmem(field, F32),
        vmem(block, F32),
        vmem(block, jnp.int32),
        vmem((32,) + block, F32),
        vmem(field, F32),
        vmem(field, F32),
        vmem(block, F32),
        vmem((SETS * 11, 12, 32, NLANE), F32),
        vmem((5, 12, 32, NLANE), F32),
        vmem((32,) + block, F32),
        vmem((32,) + block, F32),
        vmem((32,) + block, F32),
        vmem((32,) + block, F32),
        vmem((4, 22, NROW, NLANE), F32),
        vmem(field, F32),
        vmem(field, F32),
        vmem(field, F32),
        vmem(field, F32),
        vmem(block, F32),
        vmem(field, F32),
        vmem(field, F32),
        vmem(field, F32),
        vmem(block, F32),
        vmem((SETS, NROW, NLANE), F32),
        vmem((SETS, NPL, 8, NLANE), F32),
        vmem((2, SETS, 2, NLANE), F32),
        vmem((2, SETS, 6, NROW, NLANE), F32),
        vmem((2, SETS, NROW, NLANE), F32),
        vmem((2, SETS, 1, NLANE), F32),
        vmem((SETS, NPL, 8, NLANE), F32),
        vmem((2, SETS, 6, NROW, NLANE), F32),
        vmem((2, SETS, 8, NLANE), F32),
        vmem((2, 2, SETS, 2, NLANE), F32),
        vmem((2, 2, SETS, 1, NLANE), F32),
        pltpu.SemaphoreType.DMA((7,)),
        pltpu.SemaphoreType.DMA((7,)),
        pltpu.SemaphoreType.DMA((53,)),
        pltpu.SemaphoreType.DMA((53,)),
    ]
    made = pl.pallas_call(
        kernel,
        out_shape=(
            shape(field, F32),
            shape(field, F32),
            shape(field, F32),
            shape(field, F32),
            shape(block, F32),
        ),
        in_specs=[anywhere] * 5 + [pl.BlockSpec(memory_space=pltpu.SMEM)] + [anywhere] * 2,
        out_specs=[anywhere] * 5,
        scratch_shapes=scratch,
        compiler_params=pltpu.CompilerParams(
            collective_id=0, has_side_effects=True, vmem_limit_bytes=62 * 1024 * 1024
        ),
        name="rock_wall_step",
    )(
        displacement,
        velocity,
        modulus,
        classes,
        bond_integrity,
        densities,
        adjoint_disp,
        adjoint_vel,
    )
    return pl.pallas_call(
        hand_over,
        out_shape=tuple(shape(x.shape, F32) for x in made),
        in_specs=[anywhere] * 5,
        out_specs=[anywhere] * 5,
        scratch_shapes=[vmem(x.shape, F32) for x in made] + [pltpu.SemaphoreType.DMA((2, 5))],
        name="hand_over",
    )(*made)


def hand_over(*refs):
    given, outs, held, sems = refs[:5], refs[5:10], refs[10:15], refs[15]
    inward = [pltpu.make_async_copy(given[j], held[j], sems.at[0, j]) for j in range(5)]
    outward = [pltpu.make_async_copy(held[j], outs[j], sems.at[1, j]) for j in range(5)]
    for copy in inward:
        copy.start()
    for j in range(5):
        inward[j].wait()
        outward[j].start()
    for copy in outward:
        copy.wait()


def solution(mesh):
    field = P(None, "rad", "dep", "az")
    block = P("rad", "dep", "az")
    return jax.shard_map(
        shards,
        mesh=mesh,
        in_specs=(field, field, block, block, field, P(), field, field),
        out_specs=(field, field, field, field, block),
        check_vma=False,
    )
```

```python
import math

import jax
import jax.numpy as jnp
from jax import lax
from jax.experimental import pallas as pl
from jax.experimental.pallas import tpu as pltpu
from jax.sharding import PartitionSpec as P

BOND_OFFSETS = [
    (p, q, r)
    for p in range(-2, 3)
    for q in range(-2, 3)
    for r in range(-2, 3)
    if 0 < p * p + q * q + r * r <= 4
]
F32 = jnp.float32
NPL, NROW, NLANE = 8, 16, 128
DISP, CARRIED, MOVED, BACK = range(4)
SETS = 4
MESH = pl.DeviceIdType.MESH
NEIGHBOURS = [
    (da, dr, dd)
    for dd in (0, 1)
    for dr in (-1, 0, 1)
    for da in (-1, 0, 1)
    if (da, dr, dd) != (0, 0, 0)
]
FACES = [(0, -1, 0), (0, 1, 0)]
REST = sorted(
    (n for n in NEIGHBOURS if n not in FACES), key=lambda n: (-abs(n[1]), n[2] if n[1] else 0, -abs(n[0]))
)
MESSAGES = FACES + REST
PARTNER = (0, 0, 1)
NEAR = [n for n in MESSAGES if n[1] == 0 and n != PARTNER]
ALONG = [k for k, o in enumerate(BOND_OFFSETS) if o[2] == 0]
ACROSS = [k for k, o in enumerate(BOND_OFFSETS) if o[2] != 0]
RADIAL = {
    side: [n for n in MESSAGES if n[1] == (-1 if side else 1)] for side in (0, 1)
}


def size_of(offset):
    length_sq = sum(o * o for o in offset)
    mult = max(abs(o) for o in offset)
    return mult, 2.0 * mult / length_sq, mult / math.sqrt(length_sq)


def signed(offset, parts):
    total = None
    for o, part in zip(offset, parts):
        if o != 0:
            if total is None:
                total = part if o > 0 else -part
            else:
                total = total + part if o > 0 else total - part
    return total


def add_signed(offset, parts, value):
    return [
        part if o == 0 else (part + value if o > 0 else part - value)
        for o, part in zip(offset, parts)
    ]


def kernel(
    disp_h,
    vel_h,
    mod_h,
    cls_h,
    bi_h,
    dens,
    adjd_h,
    adjv_h,
    moved_h,
    newv_h,
    gdisp_h,
    gvel_h,
    gmod_h,
    disp,
    vel,
    mod,
    cls,
    bi,
    adjd,
    adjv,
    rden,
    w,
    m,
    ecoef,
    gcoef,
    acoef,
    bcoef,
    xcoef,
    force1,
    force2,
    turn2,
    turn3,
    sens,
    pack,
    sd,
    se,
    sf,
    rp,
    rpr,
    rd,
    rf,
    rdr,
    re,
    rer,
    load_sem,
    send_sem,
    recv_sem,
):
    az, rad, dep = lax.axis_index("az"), lax.axis_index("rad"), lax.axis_index("dep")
    naz, nrad = lax.axis_size("az"), lax.axis_size("rad")
    lane = lax.broadcasted_iota(jnp.int32, (NROW, NLANE), 1)
    lane_all = lax.broadcasted_iota(jnp.int32, (NPL, NROW, NLANE), 2)
    lane8_all = lax.broadcasted_iota(jnp.int32, (NPL, 8, NLANE), 2)
    lane8 = lax.broadcasted_iota(jnp.int32, (8, NLANE), 1)
    sub8 = lax.broadcasted_iota(jnp.int32, (8, NLANE), 0)

    def place(n):
        da, dr, dd = n
        return {
            "az": lax.rem(az + (da + naz), naz),
            "rad": lax.rem(rad + (dr + nrad), nrad),
            "dep": (1 - dep) if dd else dep,
        }

    barrier = pltpu.get_barrier_semaphore()
    for n in NEIGHBOURS:
        pl.semaphore_signal(barrier, inc=1, device_id=place(n), device_id_type=MESH)

    loads = {}
    for j, (name, src, dst) in enumerate(
        (
            ("disp", disp_h, disp),
            ("mod", mod_h, mod),
            ("cls", cls_h, cls),
            ("adjv", adjv_h, adjv),
            ("bi", bi_h, bi),
            ("vel", vel_h, vel),
            ("adjd", adjd_h, adjd),
        )
    ):
        loads[name] = pltpu.make_async_copy(src, dst, load_sem.at[j])
        loads[name].start()

    edge_row = 15 - 15 * dep
    second_row = 14 - 13 * dep
    halo_row = 8 + 16 - 17 * dep
    halo_row2 = 8 + 17 - 19 * dep
    blank = pl.multiple_of(24 * dep, 8)

    def clear(ref):
        ref[:, pl.ds(blank, 8), :] = jnp.zeros((12, 8, NLANE), F32)
        for plane in (0, 1, 10, 11):
            ref[plane] = jnp.zeros((32, NLANE), F32)

    def clear_w(j, carry):
        clear(w.at[j])
        return carry

    def clear_m(j, carry):
        clear(m.at[j])
        return carry

    lax.fori_loop(0, SETS * 9, clear_w, 0)
    lax.fori_loop(0, 5, clear_m, 0)
    sd[...] = jnp.zeros(sd.shape, F32)
    pack[...] = jnp.zeros(pack.shape, F32)

    def chan(t, c, r):
        return w.at[t * 9 + c * 3 + 1 + r]

    def near(t, c, offset, i):
        p, q, r = offset
        if abs(r) == 2:
            return w[SETS * 9 + t * 2 + (r > 0), i + 2, 8:24, :]
        return w[t * 9 + c * 3 + 1 + r, i + (2 + p), 8 + q : 24 + q, :]

    def near_m(offset, i):
        p, q, r = offset
        return m[2 + r, i + (2 + p), 8 + q : 24 + q, :]

    def centre(t, i):
        return [w[t * 9 + c * 3 + 1, i + 2, 8:24, :] for c in range(3)]

    def project(t, offset, i, cen):
        parts = [near(t, c, offset, i) if offset[c] else None for c in range(3)]
        return signed(offset, parts) - signed(offset, cen)

    own = pl.ds(2, NPL)

    def pack_planes(t, first, count, with_mod):
        at = pl.ds(2 + first, count)
        here = pl.ds(first, count)
        groups = None
        lanes = lane_all[:count]
        for c in range(4 if with_mod else 3):
            ref = m.at[2] if c == 3 else chan(t, c, 0)
            rolled = pltpu.roll(ref[at, 8:24, :], 4 * c + 2, 2)
            groups = rolled if c == 0 else jnp.where(lanes >= 4 * c, rolled, groups)
            sd[t, here, c : c + 1, :] = ref[at, pl.ds(8 + edge_row, 1), :]
            if c in (1, 3):
                row = 4 if c == 1 else 5
                sd[t, here, row : row + 1, :] = ref[at, pl.ds(8 + second_row, 1), :]
        packed = pack[t]
        for j in range(count):
            i = first + j
            rolled = pltpu.roll(groups[j], 16 * i, 1) if i else groups[j]
            packed = jnp.where(lane // 16 == i, rolled, packed)
        pack[t] = packed

    def pack_faces(t, with_mod, sides=(0, 1)):
        for side in sides:
            outer, inner = (9, 8) if side else (2, 3)
            for c in range(3):
                sf[side, t, c] = chan(t, c, 0)[outer, 8:24, :]
            sf[side, t, 3] = chan(t, 0, 0)[inner, 8:24, :]
            if with_mod:
                sf[side, t, 4] = m[2, outer, 8:24, :]
                sf[side, t, 5] = m[2, inner, 8:24, :]

    def pack_corners(t):
        packed = pack[t]
        for side in (0, 1):
            turned = pltpu.roll(packed, 16, 1) if side else packed
            for half in (0, 1):
                y = jnp.where(lane8 < 16, turned[8 * half : 8 * half + 8], 0.0)
                for bit in (1, 2, 4):
                    y = jnp.where((sub8 & bit) != 0, pltpu.roll(y, 16 * bit, 1), y)
                se[side, t, half : half + 1, :] = jnp.sum(y, axis=0, keepdims=True)

    def copies(phase):
        made = {}
        first, count = ((0, 2), (2, 1), (3, 1))[phase]
        sets = pl.ds(first, count)
        for j, n in enumerate(MESSAGES):
            da, dr, dd = n
            a = 0 if da == 1 else 1
            out = 1 if dr == 1 else 0
            r = 1 - out
            if da == 0 and dd == 0:
                planes = pl.ds(0, 6 if phase == 0 else 4)
                pair = sf.at[out, first, planes], rf.at[r, first, planes]
            elif da == 0 and dr == 0:
                pair = sd.at[sets], rd.at[sets]
            elif da == 0:
                plane = 7 if dr == 1 else 0
                rows = pl.ds(0, 4)
                pair = sd.at[sets, plane, rows], rdr.at[r, sets, rows]
            elif dr == 0 and dd == 0:
                pair = pack.at[sets], rp.at[a, sets]
            elif dr == 0:
                pair = pack.at[sets, pl.ds(edge_row, 1)], rpr.at[a, sets]
            elif dd == 0:
                pair = se.at[out, sets], re.at[a, r, sets]
            else:
                pair = se.at[out, sets, pl.ds(1 - dep, 1)], rer.at[a, r, sets]
            made[n] = pltpu.make_async_remote_copy(
                src_ref=pair[0],
                dst_ref=pair[1],
                send_sem=send_sem.at[phase * 17 + j],
                recv_sem=recv_sem.at[phase * 17 + j],
                device_id=place(n),
                device_id_type=MESH,
            )
        return made

    def carried_copies():
        made = {}
        for out in (0, 1):
            made[1 - out] = pltpu.make_async_remote_copy(
                src_ref=sf.at[out, CARRIED, pl.ds(0, 4)],
                dst_ref=rf.at[1 - out, CARRIED, pl.ds(0, 4)],
                send_sem=send_sem.at[51 + out],
                recv_sem=recv_sem.at[51 + out],
                device_id=place((0, 1 if out else -1, 0)),
                device_id_type=MESH,
            )
        return made

    def both(left, right, lanes):
        return jnp.where(lanes % 4 < 2, left, right)

    def shifted(value, edge, lanes, by):
        last = value.ndim - 1
        if by > 0:
            return pltpu.roll(jnp.where(lanes < by, edge, value), NLANE - by, last)
        return pltpu.roll(jnp.where(lanes >= NLANE + by, edge, value), -by, last)

    def spread(row, step, bits):
        y = jnp.broadcast_to(row, (8, NLANE))
        for bit in bits:
            turned = pltpu.roll(y, (NLANE - step * bit) % NLANE, 1)
            y = jnp.where((sub8 & bit) != 0, turned, y)
        return y

    def turn_left(value, by):
        return pltpu.roll(value, lax.rem(2 * NLANE - by, NLANE), 1)

    def turned_arrays(t, with_mod):
        for c in range(4 if with_mod else 3):
            for r in (-2, -1, 1, 2) if c >= 2 else (-1, 1):
                if c == 3:
                    yield c, r, m.at[2 + r]
                elif abs(r) == 2:
                    yield c, r, w.at[SETS * 9 + t * 2 + (r > 0)]
                else:
                    yield c, r, chan(t, c, r)

    def take_partner(t, with_mod):
        tile = rd[t]
        for c in range(4 if with_mod else 3):
            to = m.at[2] if c == 3 else chan(t, c, 0)
            to[own, pl.ds(halo_row, 1), :] = tile[:, c : c + 1]
        chan(t, 1, 0)[own, pl.ds(halo_row2, 1), :] = tile[:, 4:5]
        if with_mod:
            m[2, own, pl.ds(halo_row2, 1), :] = tile[:, 5:6]
        for c, r, to in turned_arrays(t, with_mod):
            ref = m.at[2] if c == 3 else chan(t, c, 0)
            to[own, 8:24, :] = pltpu.roll(ref[own, 8:24, :], (NLANE - r) % NLANE, 2)

    def take_sides(t, with_mod):
        sides = both(rp[0, t], rp[1, t], lane)
        sides = jnp.stack(
            [pltpu.roll(sides, NLANE - 16 * i, 1) if i else sides for i in range(NPL)]
        )
        rows = spread(both(rpr[0, t], rpr[1, t], lane8[0:1]), 4, (1, 2))
        rows = jnp.stack([pltpu.roll(rows, NLANE - 16 * i - 2, 1) for i in range(NPL)])
        for c, r, to in turned_arrays(t, with_mod):
            edge = pltpu.roll(sides, (2 * NLANE - (4 * c + 2) - r) % NLANE, 2)
            lanes = lane_all >= NLANE - r if r > 0 else lane_all < -r
            to[own, 8:24, :] = jnp.where(lanes, edge, to[own, 8:24, :])
        tile = rd[t]
        for r in (-1, 1):
            moved = shifted(tile, rows, lane8_all, r)
            for c in range(4 if with_mod else 3):
                to = m.at[2 + r] if c == 3 else chan(t, c, r)
                to[own, pl.ds(halo_row, 1), :] = moved[:, c : c + 1]

    def take_radial(t, side, with_mod):
        at, far = (10, 11) if side else (1, 0)
        there = (rad < nrad - 1) if side else (rad > 0)
        present = jnp.where(there, 1.0, 0.0).astype(F32)
        edges = [
            spread(
                both(
                    re[0, side, t, h : h + 1, :], re[1, side, t, h : h + 1, :], lane8[0:1]
                ),
                16,
                (1, 2, 4),
            )
            for h in (0, 1)
        ]
        for c in range(4 if with_mod else 3):
            value = rf[side, t, 4 if c == 3 else c]
            turned = [pltpu.roll(e, NLANE - (4 * c + 2), 1) for e in edges]
            edge = jnp.concatenate(turned, axis=0)
            for r in (-1, 0, 1):
                new = value if r == 0 else shifted(value, edge, lane, r)
                if c == 3:
                    m[2 + r, at, 8:24, :] = new * present
                else:
                    chan(t, c, r)[at, 8:24, :] = new
        chan(t, 0, 0)[far, 8:24, :] = rf[side, t, 3]
        if with_mod:
            m[2, far, 8:24, :] = rf[side, t, 5] * present
        rows = spread(both(rer[0, side, t], rer[1, side, t], lane8[0:1]), 4, (1, 2))
        edge = turn_left(rows, 16 * 7 * dep + 2)
        tile = rdr[side, t]
        for r in (-1, 0, 1):
            moved = tile if r == 0 else shifted(tile, edge, lane8, r)
            for c in range(4 if with_mod else 3):
                if c == 3:
                    m[2 + r, at, pl.ds(halo_row, 1), :] = moved[3:4] * present
                else:
                    chan(t, c, r)[at, pl.ds(halo_row, 1), :] = moved[c : c + 1]

    def bond_first(offset, i, cen, cm, intact, forces):
        mult, kappa, scale = size_of(offset)
        nm = near_m(offset, i)
        half = cm * nm / (cm + nm)
        e = intact * half * scale
        bend = jnp.tanh(kappa * project(DISP, offset, i, cen))
        push = e * bend
        g = e * half
        return add_signed(offset, forces, push), (
            e,
            g,
            kappa * (e - push * bend),
            g * bend,
        )

    def bond_second(offset, i, cen, cen_z, e, g, forces, turns, total):
        kappa = size_of(offset)[1]
        bend = jnp.tanh(kappa * project(MOVED, offset, i, cen))
        pull = project(CARRIED, offset, i, cen_z)
        push = e * bend
        stiff = kappa * (e - push * bend) * pull
        forces = add_signed(offset, forces, push)
        turns = add_signed(offset, turns, stiff)
        return forces, turns, total + g * bend * pull

    def bond_third(offset, i, cen_z, a, b, turns, total):
        pull = project(BACK, offset, i, cen_z)
        return add_signed(offset, turns, a * pull), total + b * pull

    def zeros(count):
        return [jnp.zeros((NROW, NLANE), F32) for _ in range(count)]

    def crossing(side):
        sign = 1 if side else -1
        outer, inner = (7, 6) if side else (0, 1)
        found = [(outer, k) for k, o in enumerate(BOND_OFFSETS) if o[0] == sign]
        double = BOND_OFFSETS.index((2 * sign, 0, 0))
        return found + [(outer, double), (inner, double)]

    def cross_first(side):
        for j, (i, k) in enumerate(crossing(side)):
            offset = BOND_OFFSETS[k]
            forces = [force1[c, i] for c in range(3)]
            forces, made = bond_first(
                offset, i, centre(DISP, i), m[2, i + 2, 8:24, :], bi[k, i], forces
            )
            for c in range(3):
                if offset[c]:
                    force1[c, i] = forces[c]
            for n, value in enumerate(made):
                xcoef[n, side * 11 + j] = value

    def cross_second(side):
        for j, (i, k) in enumerate(crossing(side)):
            offset = BOND_OFFSETS[k]
            x = side * 11 + j
            forces, turns, total = bond_second(
                offset,
                i,
                centre(MOVED, i),
                centre(CARRIED, i),
                xcoef[0, x],
                xcoef[1, x],
                [force2[c, i] for c in range(3)],
                [turn2[c, i] for c in range(3)],
                sens[i],
            )
            for c in range(3):
                if offset[c]:
                    force2[c, i] = forces[c]
                    turn2[c, i] = turns[c]
            sens[i] = total

    def cross_third(side):
        for j, (i, k) in enumerate(crossing(side)):
            offset = BOND_OFFSETS[k]
            x = side * 11 + j
            turns, total = bond_third(
                offset,
                i,
                centre(BACK, i),
                xcoef[2, x],
                xcoef[3, x],
                [turn3[c, i] for c in range(3)],
                sens[i],
            )
            for c in range(3):
                if offset[c]:
                    turn3[c, i] = turns[c]
            sens[i] = total

    sent = copies(0)
    sent_carried = carried_copies()
    for name in ("disp", "mod", "cls", "adjv"):
        loads[name].wait()
    m[2, own, 8:24, :] = mod[...]
    for c in range(3):
        chan(DISP, c, 0)[own, 8:24, :] = disp[c]
    kinds = cls[...]
    density = jnp.full((NPL, NROW, NLANE), dens[0])
    for level in range(1, 8):
        density = jnp.where(kinds == level, dens[level], density)
    rden[...] = 1.0 / density
    for c in range(3):
        chan(CARRIED, c, 0)[own, 8:24, :] = 0.25 * adjv[c] * rden[...]
    for t in (DISP, CARRIED):
        pack_planes(t, 0, NPL, t == DISP)
        pack_faces(t, t == DISP)
        pack_corners(t)
    pl.semaphore_wait(barrier, len(NEIGHBOURS))
    for n in MESSAGES:
        sent[n].start()
    for side in (0, 1):
        sent_carried[side].start()
    for name in ("bi", "vel", "adjd"):
        loads[name].wait()

    def sweep_first(bonds, fresh):
        def plane(i, carry):
            cen, cm = centre(DISP, i), m[2, i + 2, 8:24, :]
            forces = zeros(3) if fresh else [force1[c, i] for c in range(3)]
            for k in bonds:
                forces, made = bond_first(BOND_OFFSETS[k], i, cen, cm, bi[k, i], forces)
                for ref, value in zip((ecoef, gcoef, acoef, bcoef), made):
                    ref[k, i] = value
            for c in range(3):
                force1[c, i] = forces[c]
            return carry

        lax.fori_loop(0, NPL, plane, 0)

    sent[PARTNER].wait_recv()
    take_partner(DISP, True)
    sweep_first(ALONG, True)
    for n in NEAR:
        sent[n].wait_recv()
    take_sides(DISP, True)
    sweep_first(ACROSS, False)

    def end_first(first, count):
        here = pl.ds(first, count)
        for c in range(3):
            accel = force1[c, here] * rden[here]
            moved = disp[c, here] + 0.5 * vel[c, here] + 0.125 * accel
            chan(MOVED, c, 0)[pl.ds(2 + first, count), 8:24, :] = moved

    end_first(2, 4)
    pack_planes(MOVED, 2, 4, False)
    for n in MESSAGES:
        sent[n].wait_send()
    following = copies(1)
    for side in (0, 1):
        for n in RADIAL[side]:
            sent[n].wait_recv()
        take_radial(DISP, side, True)
        cross_first(side)
        end_first(6 * side, 2)
        pack_faces(MOVED, False, (side,))
        following[FACES[side]].start()
    sent = following

    pack_planes(MOVED, 0, 2, False)
    pack_planes(MOVED, 6, 2, False)
    pack_corners(MOVED)
    for n in REST:
        sent[n].start()
    for c in range(3):
        moved_h[c] = chan(MOVED, c, 0)[own, 8:24, :]
    sent[PARTNER].wait_recv()
    take_partner(MOVED, False)
    take_partner(CARRIED, False)
    take_sides(CARRIED, False)
    for side in (0, 1):
        sent_carried[side].wait_recv()
        sent_carried[side].wait_send()
        take_radial(CARRIED, side, False)

    def sweep_second(bonds, fresh):
        def plane(i, carry):
            cen, cen_z = centre(MOVED, i), centre(CARRIED, i)
            if fresh:
                forces, turns, total = zeros(3), zeros(3), zeros(1)[0]
            else:
                forces = [force2[c, i] for c in range(3)]
                turns = [turn2[c, i] for c in range(3)]
                total = sens[i]
            for k in bonds:
                forces, turns, total = bond_second(
                    BOND_OFFSETS[k], i, cen, cen_z, ecoef[k, i], gcoef[k, i], forces, turns, total
                )
            for c in range(3):
                force2[c, i] = forces[c]
                turn2[c, i] = turns[c]
            sens[i] = total
            return carry

        lax.fori_loop(0, NPL, plane, 0)

    sweep_second(ALONG, True)
    for n in NEAR:
        sent[n].wait_recv()
    take_sides(MOVED, False)
    sweep_second(ACROSS, False)

    def end_second(first, count):
        here = pl.ds(first, count)
        for c in range(3):
            total = adjd[c, here] + turn2[c, here]
            turn2[c, here] = total
            back = (0.25 * adjv[c, here] + 0.125 * total) * rden[here]
            chan(BACK, c, 0)[pl.ds(2 + first, count), 8:24, :] = back

    end_second(2, 4)
    pack_planes(BACK, 2, 4, False)
    for n in MESSAGES:
        sent[n].wait_send()
    following = copies(2)
    for side in (0, 1):
        for n in RADIAL[side]:
            sent[n].wait_recv()
        take_radial(MOVED, side, False)
        cross_second(side)
        end_second(6 * side, 2)
        pack_faces(BACK, False, (side,))
        following[FACES[side]].start()
    sent = following

    pack_planes(BACK, 0, 2, False)
    pack_planes(BACK, 6, 2, False)
    pack_corners(BACK)
    for n in REST:
        sent[n].start()

    for c in range(3):
        accel = (force1[c] + force2[c]) * rden[...]
        newv_h[c] = vel[c] + 0.25 * accel
        gvel_h[c] = adjv[c] + 0.5 * turn2[c]
    def sweep_third(bonds, fresh):
        def plane(i, carry):
            cen_z, total = centre(BACK, i), sens[i]
            turns = zeros(3) if fresh else [turn3[c, i] for c in range(3)]
            for k in bonds:
                turns, total = bond_third(
                    BOND_OFFSETS[k], i, cen_z, acoef[k, i], bcoef[k, i], turns, total
                )
            for c in range(3):
                turn3[c, i] = turns[c]
            sens[i] = total
            return carry

        lax.fori_loop(0, NPL, plane, 0)

    sent[PARTNER].wait_recv()
    take_partner(BACK, False)
    sweep_third(ALONG, True)
    for n in NEAR:
        sent[n].wait_recv()
    take_sides(BACK, False)
    sweep_third(ACROSS, False)

    def finish(first, count):
        here = pl.ds(first, count)
        for c in range(3):
            gdisp_h[c, here] = turn2[c, here] + turn3[c, here]
        gmod_h[here] = -sens[here] / (mod[here] * mod[here])

    finish(2, 4)
    for n in MESSAGES:
        sent[n].wait_send()
    for side in (0, 1):
        for n in RADIAL[side]:
            sent[n].wait_recv()
        take_radial(BACK, side, False)
        cross_third(side)
        finish(6 * side, 2)


def shards(
    displacement, velocity, modulus, classes, bond_integrity, densities, adjoint_disp, adjoint_vel
):
    block = (NPL, NROW, NLANE)
    field = (3,) + block
    shape = jax.ShapeDtypeStruct
    vmem = pltpu.VMEM
    anywhere = pl.BlockSpec(memory_space=pl.ANY)
    scratch = [
        vmem(field, F32),
        vmem(field, F32),
        vmem(block, F32),
        vmem(block, jnp.int32),
        vmem((32,) + block, F32),
        vmem(field, F32),
        vmem(field, F32),
        vmem(block, F32),
        vmem((SETS * 11, 12, 32, NLANE), F32),
        vmem((5, 12, 32, NLANE), F32),
        vmem((32,) + block, F32),
        vmem((32,) + block, F32),
        vmem((32,) + block, F32),
        vmem((32,) + block, F32),
        vmem((4, 22, NROW, NLANE), F32),
        vmem(field, F32),
        vmem(field, F32),
        vmem(field, F32),
        vmem(field, F32),
        vmem(block, F32),
        vmem((SETS, NROW, NLANE), F32),
        vmem((SETS, NPL, 8, NLANE), F32),
        vmem((2, SETS, 2, NLANE), F32),
        vmem((2, SETS, 6, NROW, NLANE), F32),
        vmem((2, SETS, NROW, NLANE), F32),
        vmem((2, SETS, 1, NLANE), F32),
        vmem((SETS, NPL, 8, NLANE), F32),
        vmem((2, SETS, 6, NROW, NLANE), F32),
        vmem((2, SETS, 8, NLANE), F32),
        vmem((2, 2, SETS, 2, NLANE), F32),
        vmem((2, 2, SETS, 1, NLANE), F32),
        pltpu.SemaphoreType.DMA((7,)),
        pltpu.SemaphoreType.DMA((53,)),
        pltpu.SemaphoreType.DMA((53,)),
    ]
    made = pl.pallas_call(
        kernel,
        out_shape=(
            vmem(field, F32),
            vmem(field, F32),
            vmem(field, F32),
            vmem(field, F32),
            vmem(block, F32),
        ),
        in_specs=[anywhere] * 5 + [pl.BlockSpec(memory_space=pltpu.SMEM)] + [anywhere] * 2,
        out_specs=[pl.BlockSpec(memory_space=vmem)] * 5,
        scratch_shapes=scratch,
        compiler_params=pltpu.CompilerParams(
            collective_id=0, has_side_effects=True, vmem_limit_bytes=54 * 1024 * 1024
        ),
        name="rock_wall_step",
    )(
        displacement,
        velocity,
        modulus,
        classes,
        bond_integrity,
        densities,
        adjoint_disp,
        adjoint_vel,
    )
    return pl.pallas_call(
        hand_over,
        out_shape=tuple(shape(x.shape, F32) for x in made),
        in_specs=[pl.BlockSpec(memory_space=vmem)] * 5,
        out_specs=[anywhere] * 5,
        scratch_shapes=[pltpu.SemaphoreType.DMA((5,))],
        name="hand_over",
    )(*[pltpu.with_memory_space_constraint(x, vmem) for x in made])


def hand_over(*refs):
    copies = [pltpu.make_async_copy(refs[j], refs[5 + j], refs[10].at[j]) for j in range(5)]
    for copy in copies:
        copy.start()
    for copy in copies:
        copy.wait()


def solution(mesh):
    field = P(None, "rad", "dep", "az")
    block = P("rad", "dep", "az")
    return jax.shard_map(
        shards,
        mesh=mesh,
        in_specs=(field, field, block, block, field, P(), field, field),
        out_specs=(field, field, field, field, block),
        check_vma=False,
    )
```
